256 devices in a mesh: seq: 32 (over x, z_lo, core), tp: 8 (over y, z_hi).
Axes of the slice: x: 4, y: 4, z: 8 (z_hi: 2, z_lo: 4; z = z_hi * 4 + z_lo), core: 2. Of those that a mesh axis runs over, the one named last changes fastest.
Arguments:
- inner_gate: bfloat16 [8192, 8192], P('seq', 'tp'), may hold values from -6 to 6
- values: bfloat16 [8192, 8192], P('seq', 'tp'), may hold values from -6 to 6
- outer_gate: bfloat16 [8192, 8192], P('seq', 'tp'), may hold values from -6 to 6
- filters: float32 [8192, 8192], P('seq', 'tp'), may hold values from -0.0625 to 0.0625
- skip_gain: float32 [8192], P('tp'), may hold values from 0.5 to 2
- w_out: bfloat16 [8192, 4096], P('tp'), may hold values from -0.09375 to 0.09375
Outputs:
- mixed_out: bfloat16 [8192, 4096], P('seq', 'tp')
The draws below stay inside these ranges and needn't reach their ends.
All inputs are finite; a program needn't handle non-finite values.
Results may differ from the reference program's by a relative error of at most 0.015.
Values may be sent and summed in bfloat16 or wider, within the bound.
A program may use at most 192 MiB of HBM per device.

```python
import jax
import jax.numpy as jnp

C = 8192
D = 4096
TOKENS = 8192
N_TP = 8


def spiked(entries, key, source, target, parts, factor):
    def block_of(axis_at):
        return (jnp.arange(entries.shape[axis_at]) // (entries.shape[axis_at] // parts)).reshape((-1,) + (1,) * (entries.ndim - 1 - axis_at))

    first = jax.random.permutation(key, parts)[block_of(target)]
    far = (block_of(target) + parts // 2) % parts
    return jnp.where((block_of(source) == first) | (block_of(source) == far), factor * entries, entries)


def shard_levels(rng, extent, split, smallest, high):
    def one(dim, parts):
        heights = jax.random.uniform(jax.random.fold_in(jax.random.fold_in(rng, 6), dim), (parts,), jnp.float32, smallest / len(split), high / len(split))
        return jnp.repeat(jnp.exp(heights), extent[dim] // parts).reshape((-1,) + (1,) * (len(extent) - dim - 1))

    loudness = one(*split[0])
    for cut in split[1:]:
        loudness = loudness * one(*cut)
    return loudness


def noise(stream_key, shape, scale, limit, cuts=(), held_as=jnp.bfloat16):
    array = scale * jax.random.normal(stream_key, shape, jnp.float32)
    if cuts:
        array = array * shard_levels(stream_key, shape, cuts, -0.22, 0.18)
    return jnp.clip(array, -limit, limit).astype(held_as)


def bell_draw_with(key, shape, width, limit, shards, heavy, held_as=jnp.bfloat16):
    result = width * jax.random.normal(key, shape, jnp.float32)
    if shards:
        result = result * shard_levels(key, shape, shards, -0.22, 0.18)
    return jnp.clip(spiked(result, jax.random.fold_in(key, 3), *heavy), -limit, limit).astype(held_as)


def setup_inputs(seed: int = 0) -> dict:
    key_list = jax.random.split(jax.random.key(seed), 7)
    return {
        "inner_gate": noise(key_list[0], (TOKENS, C), 1.0, 6.0, ((0, 32), (1, 8))),
        "values": noise(key_list[1], (TOKENS, C), 1.0, 6.0, ((0, 32), (1, 8))),
        "outer_gate": noise(key_list[2], (TOKENS, C), 1.0, 6.0, ((0, 32), (1, 8))),
        "filters": noise(key_list[3], (TOKENS, C), TOKENS ** -0.5, 0.0625, ((0, 32), (1, 8)), jnp.float32),
        "skip_gain": jnp.clip(0.5 + 1.5 * jax.random.uniform(key_list[4], (C,), jnp.float32) ** shard_levels(key_list[4], (C,), ((0, 8),), -0.2, 0.2), 0.5, 2.0),
        "w_out": bell_draw_with(key_list[5], (C, D), C ** -0.5, 0.09375, ((0, 8),), (0, 1, 8, 2.0)),
    }


def reference(inner_gate, values, outer_gate, filters, skip_gain, w_out):
    product = inner_gate.astype(jnp.float32) * values.astype(jnp.float32)
    length = product.shape[0]
    product_spec = jnp.fft.rfft(product, n=2 * length, axis=0)
    filter_spec = jnp.fft.rfft(filters, n=2 * length, axis=0)
    conv = jnp.fft.irfft(product_spec * filter_spec, n=2 * length, axis=0)[:length]
    mixed = (outer_gate.astype(jnp.float32) * (conv + skip_gain[None, :] * product)).astype(jnp.bfloat16)
    group = C // N_TP
    total = jnp.zeros((length, D), jnp.float32)
    for index in range(N_TP):
        partial_sum = jnp.dot(mixed[:, index * group:(index + 1) * group], w_out[index * group:(index + 1) * group], preferred_element_type=jnp.float32)
        total = total + partial_sum.astype(jnp.bfloat16).astype(jnp.float32)
    return total.astype(jnp.bfloat16)
```

```python
import math

import jax
import jax.numpy as jnp
import numpy as np
from jax import lax
from jax.experimental import pallas as pl
from jax.experimental.pallas import tpu as pltpu
from jax.sharding import PartitionSpec as P

MESH = pl.DeviceIdType.MESH
NT = (((1,), (1,)), ((), ()))
SEQ = 32
CHAN = 32
FINE = 256
BINS = 33
LENGTH = 2 * SEQ * FINE


def twist(z, angle):
    c, s = math.cos(angle), math.sin(angle)
    re, im = z
    if abs(s) < 1e-9:
        return (re, im) if c > 0 else (-re, -im)
    if abs(c) < 1e-9:
        return (-im, re) if s > 0 else (im, -re)
    if abs(abs(c) - abs(s)) < 1e-9:
        a = abs(c)
        d, e = (re - im) * a, (re + im) * a
        if c > 0:
            return (d, e) if s > 0 else (e, -d)
        return (-e, d) if s > 0 else (-d, -e)
    return (re * c - im * s, re * s + im * c)


def cadd(a, b):
    return (a[0] + b[0], a[1] + b[1])


def csub(a, b):
    return (a[0] - b[0], a[1] - b[1])


def complex_dft(z, sign):
    n = len(z)
    if n == 1:
        return z
    even, odd = complex_dft(z[0::2], sign), complex_dft(z[1::2], sign)
    first, second = [], []
    for k in range(n // 2):
        t = twist(odd[k], sign * 2 * math.pi * k / n)
        first.append(cadd(even[k], t))
        second.append(csub(even[k], t))
    return first + second


def odd_bins(v):
    n = 2 * len(v)
    q = n // 4
    z = [twist((v[p], -v[p + q]), -2 * math.pi * p / n) for p in range(q)]
    bins = {}
    for r, value in enumerate(complex_dft(z, -1)):
        k = 4 * r + 1
        bins[k if k <= n // 2 else n - k] = value if k <= n // 2 else (value[0], -value[1])
    return bins


def real_dft(x):
    n = len(x)
    if n == 2:
        return {0: (x[0] + x[1], None), 1: (x[0] - x[1], None)}
    h = n // 2
    bins = {2 * k: value for k, value in real_dft([x[p] + x[p + h] for p in range(h)]).items()}
    bins.update(odd_bins([x[p] - x[p + h] for p in range(h)]))
    return bins


def padded_real_dft(x):
    bins = {2 * k: value for k, value in real_dft(x).items()}
    bins.update(odd_bins(x))
    return bins


def odd_back(bins, n):
    q = n // 4
    z = []
    for r in range(q):
        k = 4 * r + 1
        z.append(bins[k] if k <= n // 2 else (bins[n - k][0], -bins[n - k][1]))
    d = [twist(c, 2 * math.pi * p / n) for p, c in enumerate(complex_dft(z, 1))]
    return [a for a, _ in d] + [-b for _, b in d]


def real_back(bins, n):
    if n == 2:
        return [bins[0][0] + bins[1][0], bins[0][0] - bins[1][0]]
    u = real_back({k // 2: value for k, value in bins.items() if k % 2 == 0}, n // 2)
    v = odd_back(bins, n)
    return [a + b for a, b in zip(u, v)] + [a - b for a, b in zip(u, v)]


def half_real_back(bins, n):
    u = real_back({k // 2: value for k, value in bins.items() if k % 2 == 0}, n // 2)
    return [a + b for a, b in zip(u, odd_back(bins, n))]


def tables():
    idx = np.arange(FINE)
    ang = 2 * np.pi * ((idx[:, None] * idx[None, :]) % FINE) / FINE
    c, s = np.cos(ang), np.sin(ang)
    forward = np.block([[c, -s], [s, c]])
    back = np.block([[c, s], [-s, c]])
    tw = 2 * np.pi * np.arange(BINS)[:, None] * idx[None, :] / LENGTH
    scale = np.full((BINS, 1), 2.0 / LENGTH)
    scale[0] = scale[-1] = 1.0 / LENGTH
    twiddle = np.stack([np.cos(tw), np.sin(tw), np.cos(tw) * scale, np.sin(tw) * scale], 1)
    return (
        jnp.asarray(forward, jnp.bfloat16),
        jnp.asarray(back, jnp.bfloat16),
        jnp.asarray(twiddle, jnp.float32),
    )


def identity():
    row = lax.broadcasted_iota(jnp.int32, (FINE, FINE), 0)
    col = lax.broadcasted_iota(jnp.int32, (FINE, FINE), 1)
    return jnp.where(row == col, 1.0, 0.0).astype(jnp.bfloat16)


def spread_kernel(inner, values, filters, recv, send, eye, send_sem, recv_sem):
    me = lax.axis_index("seq")
    barrier = pltpu.get_barrier_semaphore()

    @pl.loop(1, SEQ)
    def _(i):
        pl.semaphore_signal(barrier, inc=1, device_id={"seq": me ^ i}, device_id_type=MESH)

    eye[...] = identity()
    pl.semaphore_wait(barrier, SEQ - 1)

    @pl.loop(0, 4)
    def _(step):
        block = lax.rem(me // 8 + 1 + step, 4)
        cols = pl.ds(pl.multiple_of(block * FINE, FINE), FINE)
        product = (inner[:, cols].astype(jnp.float32) * values[:, cols].astype(jnp.float32)).astype(jnp.bfloat16)
        for half, part in enumerate((product, filters[:, cols].astype(jnp.bfloat16))):
            turned = lax.dot_general(eye[...], part, NT, preferred_element_type=jnp.float32)
            send[pl.ds(block * 8, 8), half * CHAN : (half + 1) * CHAN, :] = turned.astype(jnp.bfloat16).reshape(8, CHAN, FINE)

        @pl.loop(0, 8)
        def _(i):
            peer = block * 8 + (lax.rem(me, 8) ^ (7 - i))

            @pl.when(peer != me)
            def _():
                pltpu.make_async_remote_copy(
                    send.at[peer], recv.at[me], send_sem, recv_sem, device_id={"seq": peer}, device_id_type=MESH
                ).start()

    recv[me] = send[me]
    pltpu.make_async_copy(send.at[pl.ds(0, SEQ - 1)], send.at[pl.ds(0, SEQ - 1)], send_sem).wait()
    pltpu.make_async_copy(recv.at[pl.ds(0, SEQ - 1)], recv.at[pl.ds(0, SEQ - 1)], recv_sem).wait()


def spread(inner, values, filters):
    vmem = pl.BlockSpec(memory_space=pltpu.VMEM)
    return pl.pallas_call(
        spread_kernel,
        out_shape=jax.ShapeDtypeStruct((SEQ, 2 * CHAN, FINE), jnp.bfloat16),
        in_specs=[vmem] * 3,
        out_specs=vmem,
        scratch_shapes=[
            pltpu.VMEM((SEQ, 2 * CHAN, FINE), jnp.bfloat16),
            pltpu.VMEM((FINE, FINE), jnp.bfloat16),
            pltpu.SemaphoreType.DMA,
            pltpu.SemaphoreType.DMA,
        ],
        compiler_params=pltpu.CompilerParams(collective_id=0, has_side_effects=True, vmem_limit_bytes=40 * 2**20),
        name="spread",
    )(inner, values, filters)


def conv_kernel(block, forward, back, twiddle, out, spec, waves):
    f32 = jnp.float32

    @pl.loop(0, 4)
    def _(group):
        rows = pl.ds(pl.multiple_of(group * 16, 16), 16)
        for lane in range(2):
            lanes = slice(lane * 128, lane * 128 + 128)
            bins = padded_real_dft([block[p, rows, lanes].astype(f32) for p in range(SEQ)])
            for k, (re, im) in bins.items():
                c, s = twiddle[k, 0:1, lanes], twiddle[k, 1:2, lanes]
                if im is None:
                    a, b = re * c, -(re * s)
                else:
                    a, b = re * c + im * s, im * c - re * s
                spec[k, rows, lanes] = a.astype(jnp.bfloat16)
                spec[k, rows, lane * 128 + FINE : lane * 128 + FINE + 128] = b.astype(jnp.bfloat16)

    group_bins = 11

    @pl.loop(0, BINS // group_bins)
    def _(step):
        at = pl.ds(step * group_bins, group_bins)
        both = jnp.dot(
            spec[at].reshape(group_bins * 2 * CHAN, 2 * FINE), forward[...], preferred_element_type=f32
        ).reshape(group_bins, 2, CHAN, 2 * FINE)
        zr, zi = both[:, 0, :, :FINE], both[:, 0, :, FINE:]
        hr, hi = both[:, 1, :, :FINE], both[:, 1, :, FINE:]
        y = jnp.concatenate([zr * hr - zi * hi, zr * hi + zi * hr], axis=-1).astype(jnp.bfloat16)
        waves[at] = jnp.dot(
            y.reshape(group_bins * CHAN, 2 * FINE), back[...], preferred_element_type=f32
        ).reshape(group_bins, CHAN, 2 * FINE)

    @pl.loop(0, 2)
    def _(group):
        rows = pl.ds(pl.multiple_of(group * 16, 16), 16)
        for lane in range(2):
            lanes = slice(lane * 128, lane * 128 + 128)
            bins = {}
            for k in range(BINS):
                re, im = waves[k, rows, lanes], waves[k, rows, lane * 128 + FINE : lane * 128 + FINE + 128]
                c, s = twiddle[k, 2:3, lanes], twiddle[k, 3:4, lanes]
                bins[k] = (re * c - im * s, None if k in (0, BINS - 1) else im * c + re * s)
            for p, y in enumerate(half_real_back(bins, 2 * SEQ)):
                out[p, rows, lanes] = y.astype(jnp.bfloat16)


def convolve(block):
    vmem = pl.BlockSpec(memory_space=pltpu.VMEM)
    return pl.pallas_call(
        conv_kernel,
        out_shape=jax.ShapeDtypeStruct((SEQ, CHAN, FINE), jnp.bfloat16),
        in_specs=[vmem] * 4,
        out_specs=vmem,
        scratch_shapes=[
            pltpu.VMEM((BINS, 2 * CHAN, 2 * FINE), jnp.bfloat16),
            pltpu.VMEM((BINS, CHAN, 2 * FINE), jnp.float32),
        ],
        compiler_params=pltpu.CompilerParams(vmem_limit_bytes=40 * 2**20),
        name="convolve",
    )(block, *tables())


def project_kernel(
    conv, inner, values, outer, skip, w_hbm, out,
    turned, mixed, eye, w, psend, precv, kept, zsend, zrecv,
    w_sem, send_sem, recv_sem, psend_sem, precv_sem, zsend_sem, zrecv_sem,
):
    f32 = jnp.float32
    me, tp = lax.axis_index("seq"), lax.axis_index("tp")
    y, z = tp // 2, lax.rem(tp, 2)
    load = pltpu.make_async_copy(w_hbm, w, w_sem)
    load.start()
    barrier = pltpu.get_barrier_semaphore()

    @pl.loop(1, SEQ)
    def _(i):
        pl.semaphore_signal(barrier, inc=1, device_id={"seq": me ^ i}, device_id_type=MESH)

    for d in range(1, 4):
        pl.semaphore_signal(barrier, inc=1, device_id={"tp": lax.rem(y + d, 4) * 2 + z}, device_id_type=MESH)
    pl.semaphore_signal(barrier, inc=1, device_id={"tp": y * 2 + 1 - z}, device_id_type=MESH)
    eye[...] = identity()
    pl.semaphore_wait(barrier, SEQ + 3)

    @pl.loop(1, SEQ)
    def _(i):
        peer = me ^ (SEQ - i)
        pltpu.make_async_remote_copy(
            conv.at[peer], turned.at[me], send_sem, recv_sem, device_id={"seq": peer}, device_id_type=MESH
        ).start()

    turned[me] = conv[me]
    pltpu.make_async_copy(conv.at[pl.ds(0, SEQ - 1)], conv.at[pl.ds(0, SEQ - 1)], send_sem).wait()
    pltpu.make_async_copy(turned.at[pl.ds(0, SEQ - 1)], turned.at[pl.ds(0, SEQ - 1)], recv_sem).wait()

    @pl.loop(0, 4)
    def _(block):
        cols = pl.ds(pl.multiple_of(block * FINE, FINE), FINE)
        part = turned[pl.ds(block * 8, 8)].reshape(FINE, FINE)
        here = lax.dot_general(eye[...], part, NT, preferred_element_type=f32)
        product = inner[:, cols].astype(f32) * values[:, cols].astype(f32)
        mixed[:, cols] = (outer[:, cols].astype(f32) * (here + skip[:, cols] * product)).astype(jnp.bfloat16)

    load.wait()

    def shares(chunk, d):
        target = lax.rem(y + d, 4)
        return pltpu.make_async_remote_copy(
            psend.at[chunk, d], precv.at[chunk, d], psend_sem.at[chunk, d], precv_sem.at[chunk, d],
            device_id={"tp": target * 2 + z}, device_id_type=MESH,
        )

    def swap(chunk):
        return pltpu.make_async_remote_copy(
            zsend.at[chunk], zrecv.at[chunk], zsend_sem.at[chunk], zrecv_sem.at[chunk],
            device_id={"tp": y * 2 + 1 - z}, device_id_type=MESH,
        )

    for chunk in range(2):
        rows = slice(chunk * 128, chunk * 128 + 128)
        for d in (2, 1, 3, 0):
            target = lax.rem(y + d, 4)

            @pl.loop(0, 2)
            def _(part):
                cols = pl.ds(pl.multiple_of(target * 1024 + part * 512, 512), 512)
                psend[chunk, d, :, pl.ds(pl.multiple_of(part * 512, 512), 512)] = jnp.dot(
                    mixed[rows, :], w[:, cols], preferred_element_type=f32
                ).astype(jnp.bfloat16)

            if d:
                shares(chunk, d).start()

    for chunk in range(2):
        for d in range(1, 4):
            shares(chunk, d).wait_recv()

        def total(half):
            cols = pl.ds(pl.multiple_of(half * 512, 512), 512)
            acc = psend[chunk, 0, :, cols].astype(f32)
            for d in range(1, 4):
                acc += precv[chunk, d, :, cols].astype(f32)
            return acc

        zsend[chunk] = total(1 - z).astype(jnp.bfloat16)
        swap(chunk).start()
        kept[chunk] = total(z)

    for chunk in range(2):
        swap(chunk).wait()
        out[chunk * 128 : chunk * 128 + 128, :] = (kept[chunk] + zrecv[chunk].astype(f32)).astype(jnp.bfloat16)
        for d in range(1, 4):
            shares(chunk, d).wait_send()


def project(conv, inner, values, outer, skip, w_out):
    vmem = pl.BlockSpec(memory_space=pltpu.VMEM)
    bf16 = jnp.bfloat16
    return pl.pallas_call(
        project_kernel,
        out_shape=jax.ShapeDtypeStruct((FINE, 512), bf16),
        in_specs=[vmem] * 5 + [pl.BlockSpec(memory_space=pl.ANY)],
        out_specs=vmem,
        scratch_shapes=[
            pltpu.VMEM((SEQ, CHAN, FINE), bf16),
            pltpu.VMEM((FINE, 1024), bf16),
            pltpu.VMEM((FINE, FINE), bf16),
            pltpu.VMEM((1024, 4096), bf16),
            pltpu.VMEM((2, 4, 128, 1024), bf16),
            pltpu.VMEM((2, 4, 128, 1024), bf16),
            pltpu.VMEM((2, 128, 512), jnp.float32),
            pltpu.VMEM((2, 128, 512), bf16),
            pltpu.VMEM((2, 128, 512), bf16),
            pltpu.SemaphoreType.DMA,
            pltpu.SemaphoreType.DMA,
            pltpu.SemaphoreType.DMA,
            pltpu.SemaphoreType.DMA((2, 4)),
            pltpu.SemaphoreType.DMA((2, 4)),
            pltpu.SemaphoreType.DMA((2,)),
            pltpu.SemaphoreType.DMA((2,)),
        ],
        compiler_params=pltpu.CompilerParams(collective_id=1, has_side_effects=True, vmem_limit_bytes=50 * 2**20),
        name="project",
    )(conv, inner, values, outer, skip.reshape(1, -1), w_out)


def local(inner_gate, values, outer_gate, filters, skip_gain, w_out):
    block = spread(inner_gate, values, filters)
    conv = convolve(block)
    return project(conv, inner_gate, values, outer_gate, skip_gain, w_out)


def solution(mesh):
    in_specs = (P("seq", "tp"), P("seq", "tp"), P("seq", "tp"), P("seq", "tp"), P("tp"), P("tp", None))
    return jax.shard_map(local, mesh=mesh, in_specs=in_specs, out_specs=P("seq", "tp"), check_vma=False)
```

```python
import math

import jax
import jax.numpy as jnp
import numpy as np
from jax import lax
from jax.experimental import pallas as pl
from jax.experimental.pallas import tpu as pltpu
from jax.sharding import PartitionSpec as P

MESH = pl.DeviceIdType.MESH
NT = (((1,), (1,)), ((), ()))
SEQ = 32
PART = 16
FINE = 256
BINS = 33
LENGTH = 2 * SEQ * FINE


def twist(z, angle):
    c, s = math.cos(angle), math.sin(angle)
    re, im = z
    if abs(s) < 1e-9:
        return (re, im) if c > 0 else (-re, -im)
    if abs(c) < 1e-9:
        return (-im, re) if s > 0 else (im, -re)
    if abs(abs(c) - abs(s)) < 1e-9:
        a = abs(c)
        d, e = (re - im) * a, (re + im) * a
        if c > 0:
            return (d, e) if s > 0 else (e, -d)
        return (-e, d) if s > 0 else (-d, -e)
    return (re * c - im * s, re * s + im * c)


def cadd(a, b):
    return (a[0] + b[0], a[1] + b[1])


def csub(a, b):
    return (a[0] - b[0], a[1] - b[1])


def complex_dft(z, sign):
    n = len(z)
    if n == 1:
        return z
    even, odd = complex_dft(z[0::2], sign), complex_dft(z[1::2], sign)
    first, second = [], []
    for k in range(n // 2):
        t = twist(odd[k], sign * 2 * math.pi * k / n)
        first.append(cadd(even[k], t))
        second.append(csub(even[k], t))
    return first + second


def odd_bins(v):
    n = 2 * len(v)
    q = n // 4
    z = [twist((v[p], -v[p + q]), -2 * math.pi * p / n) for p in range(q)]
    bins = {}
    for r, value in enumerate(complex_dft(z, -1)):
        k = 4 * r + 1
        bins[k if k <= n // 2 else n - k] = value if k <= n // 2 else (value[0], -value[1])
    return bins


def real_dft(x):
    n = len(x)
    if n == 2:
        return {0: (x[0] + x[1], None), 1: (x[0] - x[1], None)}
    h = n // 2
    bins = {2 * k: value for k, value in real_dft([x[p] + x[p + h] for p in range(h)]).items()}
    bins.update(odd_bins([x[p] - x[p + h] for p in range(h)]))
    return bins


def padded_real_dft(x):
    bins = {2 * k: value for k, value in real_dft(x).items()}
    bins.update(odd_bins(x))
    return bins


def odd_back(bins, n):
    q = n // 4
    z = []
    for r in range(q):
        k = 4 * r + 1
        z.append(bins[k] if k <= n // 2 else (bins[n - k][0], -bins[n - k][1]))
    d = [twist(c, 2 * math.pi * p / n) for p, c in enumerate(complex_dft(z, 1))]
    return [a for a, _ in d] + [-b for _, b in d]


def real_back(bins, n):
    if n == 2:
        return [bins[0][0] + bins[1][0], bins[0][0] - bins[1][0]]
    u = real_back({k // 2: value for k, value in bins.items() if k % 2 == 0}, n // 2)
    v = odd_back(bins, n)
    return [a + b for a, b in zip(u, v)] + [a - b for a, b in zip(u, v)]


def half_real_back(bins, n):
    u = real_back({k // 2: value for k, value in bins.items() if k % 2 == 0}, n // 2)
    return [a + b for a, b in zip(u, odd_back(bins, n))]


def tables():
    idx = np.arange(FINE)
    ang = 2 * np.pi * ((idx[:, None] * idx[None, :]) % FINE) / FINE
    c, s = np.cos(ang), np.sin(ang)
    forward = np.block([[c, -s], [s, c]])
    back = np.block([[c, s], [-s, c]])
    tw = 2 * np.pi * np.arange(BINS)[:, None] * idx[None, :] / LENGTH
    scale = np.full((BINS, 1), 2.0 / LENGTH)
    scale[0] = scale[-1] = 1.0 / LENGTH
    twiddle = np.stack([np.cos(tw), np.sin(tw), np.cos(tw) * scale, np.sin(tw) * scale], 1)
    return (
        jnp.asarray(forward, jnp.bfloat16),
        jnp.asarray(back, jnp.bfloat16),
        jnp.asarray(twiddle, jnp.float32),
    )


def identity():
    row = lax.broadcasted_iota(jnp.int32, (FINE, FINE), 0)
    col = lax.broadcasted_iota(jnp.int32, (FINE, FINE), 1)
    return jnp.where(row == col, 1.0, 0.0).astype(jnp.bfloat16)


def transform(part, recv, forward, back, twiddle, spec, waves, conv):
    f32 = jnp.float32
    bf16 = jnp.bfloat16
    for kind in range(2):
        for lane in range(2):
            lanes = slice(lane * 128, lane * 128 + 128)
            bins = padded_real_dft([recv[part, p, kind, :, lanes].astype(f32) for p in range(SEQ)])
            for k, (re, im) in bins.items():
                c, s = twiddle[k, 0:1, lanes], twiddle[k, 1:2, lanes]
                if im is None:
                    a, b = re * c, -(re * s)
                else:
                    a, b = re * c + im * s, im * c - re * s
                spec[k, kind, :, lanes] = a.astype(bf16)
                spec[k, kind, :, lane * 128 + FINE : lane * 128 + FINE + 128] = b.astype(bf16)

    group = 11

    @pl.loop(0, BINS // group)
    def _(step):
        at = pl.ds(step * group, group)
        both = jnp.dot(
            spec[at].reshape(group * 2 * PART, 2 * FINE), forward[...], preferred_element_type=f32
        ).reshape(group, 2, PART, 2 * FINE)
        zr, zi = both[:, 0, :, :FINE], both[:, 0, :, FINE:]
        hr, hi = both[:, 1, :, :FINE], both[:, 1, :, FINE:]
        y = jnp.concatenate([zr * hr - zi * hi, zr * hi + zi * hr], axis=-1).astype(bf16)
        waves[at] = jnp.dot(y.reshape(group * PART, 2 * FINE), back[...], preferred_element_type=f32).reshape(
            group, PART, 2 * FINE
        )

    for lane in range(2):
        lanes = slice(lane * 128, lane * 128 + 128)
        bins = {}
        for k in range(BINS):
            re, im = waves[k, :, lanes], waves[k, :, lane * 128 + FINE : lane * 128 + FINE + 128]
            c, s = twiddle[k, 2:3, lanes], twiddle[k, 3:4, lanes]
            bins[k] = (re * c - im * s, None if k in (0, BINS - 1) else im * c + re * s)
        for p, y in enumerate(half_real_back(bins, 2 * SEQ)):
            conv[lane, part, p] = y.astype(bf16)


def kernel(
    inner_hbm, values_hbm, outer_hbm, filters_hbm, skip_hbm, w_hbm, forward_hbm, back_hbm, twiddle_hbm, out,
    inner, values, outer, filters, skip, w, forward, back, twiddle,
    send, recv, spec, waves, conv, turned, mixed, eye, psend, precv, kept, zsend, zrecv,
    load_sem, send_sem, recv_sem, csend_sem, crecv_sem, psend_sem, precv_sem, zsend_sem, zrecv_sem,
):
    f32 = jnp.float32
    bf16 = jnp.bfloat16
    me, tp = lax.axis_index("seq"), lax.axis_index("tp")
    y, z = tp // 2, lax.rem(tp, 2)
    loads = [
        pltpu.make_async_copy(a, b, load_sem.at[i])
        for i, (a, b) in enumerate((
            (inner_hbm, inner), (values_hbm, values), (filters_hbm, filters), (forward_hbm, forward), (back_hbm, back),
            (twiddle_hbm, twiddle), (outer_hbm, outer), (skip_hbm, skip), (w_hbm, w),
        ))
    ]
    for load in loads:
        load.start()
    barrier = pltpu.get_barrier_semaphore()

    @pl.loop(1, SEQ)
    def _(i):
        pl.semaphore_signal(barrier, inc=1, device_id={"seq": me ^ i}, device_id_type=MESH)

    for d in range(1, 4):
        pl.semaphore_signal(barrier, inc=1, device_id={"tp": lax.rem(y + d, 4) * 2 + z}, device_id_type=MESH)
    pl.semaphore_signal(barrier, inc=1, device_id={"tp": y * 2 + 1 - z}, device_id_type=MESH)
    row = lax.broadcasted_iota(jnp.int32, (FINE, FINE), 0)
    col = lax.broadcasted_iota(jnp.int32, (FINE, FINE), 1)
    eye[...] = jnp.where(row == col, 1.0, 0.0).astype(bf16)
    for load in loads[:3]:
        load.wait()
    pl.semaphore_wait(barrier, SEQ + 3)

    def spread(part, block):
        @pl.loop(0, 8)
        def _(i):
            peer = block * 8 + (lax.rem(me, 8) ^ (7 - i))

            @pl.when(peer != me)
            def _():
                pltpu.make_async_remote_copy(
                    send.at[part, peer], recv.at[part, me], send_sem.at[part], recv_sem.at[part],
                    device_id={"seq": peer}, device_id_type=MESH,
                ).start()

    @pl.loop(0, 4)
    def _(step):
        block = lax.rem(me // 8 + 1 + step, 4)
        cols = pl.ds(pl.multiple_of(block * FINE, FINE), FINE)
        product = (inner[:, cols].astype(f32) * values[:, cols].astype(f32)).astype(bf16)
        for kind, piece in enumerate((product, filters[:, cols].astype(bf16))):
            flat = lax.dot_general(eye[...], piece, NT, preferred_element_type=f32).astype(bf16).reshape(8, 2, PART, FINE)
            for part in range(2):
                send[part, pl.ds(block * 8, 8), kind] = flat[:, part]
        spread(0, block)

    @pl.loop(0, 4)
    def _(step):
        spread(1, lax.rem(me // 8 + 1 + step, 4))

    for part in range(2):
        recv[part, me] = send[part, me]
    for load in loads[3:6]:
        load.wait()

    def give_back(half, part):
        @pl.loop(1, SEQ)
        def _(i):
            peer = me ^ (SEQ - i)
            pltpu.make_async_remote_copy(
                conv.at[half, part, peer], turned.at[half, part, me], csend_sem.at[half, part], crecv_sem.at[half, part],
                device_id={"seq": peer}, device_id_type=MESH,
            ).start()

        turned[half, part, me] = conv[half, part, me]

    def wait_bytes(ref, sem):
        pltpu.make_async_copy(ref.at[pl.ds(0, SEQ - 1)], ref.at[pl.ds(0, SEQ - 1)], sem).wait()

    @pl.loop(0, 2)
    def _(part):
        wait_bytes(recv.at[part], recv_sem.at[part])

        @pl.when(part == 1)
        def _():
            give_back(0, 0)

        transform(part, recv, forward, back, twiddle, spec, waves, conv)

    give_back(0, 1)
    give_back(1, 0)
    give_back(1, 1)
    for load in loads[6:]:
        load.wait()

    def mix(half):
        for part in range(2):
            wait_bytes(turned.at[half, part], crecv_sem.at[half, part])
        rows = slice(half * 128, half * 128 + 128)

        @pl.loop(0, 4)
        def _(block):
            cols = pl.ds(pl.multiple_of(block * FINE, FINE), FINE)
            both = [turned[half, part, pl.ds(block * 8, 8)].reshape(8, 1, PART, 128) for part in range(2)]
            piece = jnp.concatenate(both, axis=1).reshape(FINE, 128)
            here = lax.dot_general(eye[:128, :128], piece, NT, preferred_element_type=f32)
            product = inner[rows, cols].astype(f32) * values[rows, cols].astype(f32)
            mixed[rows, cols] = (outer[rows, cols].astype(f32) * (here + skip[:, cols] * product)).astype(bf16)

    def shares(chunk, d):
        return pltpu.make_async_remote_copy(
            psend.at[chunk, d], precv.at[chunk, d], psend_sem.at[chunk, d], precv_sem.at[chunk, d],
            device_id={"tp": lax.rem(y + d, 4) * 2 + z}, device_id_type=MESH,
        )

    def swap(chunk):
        return pltpu.make_async_remote_copy(
            zsend.at[chunk], zrecv.at[chunk], zsend_sem.at[chunk], zrecv_sem.at[chunk],
            device_id={"tp": y * 2 + 1 - z}, device_id_type=MESH,
        )

    def produce(chunk):
        rows = slice(chunk * 64, chunk * 64 + 64)
        for d in (2, 1, 3, 0):
            target = lax.rem(y + d, 4)

            @pl.loop(0, 2)
            def _(piece):
                cols = pl.ds(pl.multiple_of(target * 1024 + piece * 512, 512), 512)
                psend[chunk, d, :, pl.ds(pl.multiple_of(piece * 512, 512), 512)] = jnp.dot(
                    mixed[rows, :], w[:, cols], preferred_element_type=f32
                ).astype(bf16)

            if d:
                shares(chunk, d).start()

    def add_up(chunk):
        for d in range(1, 4):
            shares(chunk, d).wait_recv()

        def total(half):
            cols = pl.ds(pl.multiple_of(half * 512, 512), 512)
            acc = psend[chunk, 0, :, cols].astype(f32)
            for d in range(1, 4):
                acc += precv[chunk, d, :, cols].astype(f32)
            return acc

        zsend[chunk] = total(1 - z).astype(bf16)
        swap(chunk).start()
        kept[chunk] = total(z)

    def finish(chunk):
        swap(chunk).wait()
        out[chunk * 64 : chunk * 64 + 64, :] = (kept[chunk] + zrecv[chunk].astype(f32)).astype(bf16)
        for d in range(1, 4):
            shares(chunk, d).wait_send()

    mix(0)
    produce(0)
    produce(1)
    mix(1)
    produce(2)
    add_up(0)
    produce(3)
    add_up(1)
    add_up(2)
    finish(0)
    add_up(3)
    finish(1)
    finish(2)
    finish(3)
    for part in range(2):
        wait_bytes(send.at[part], send_sem.at[part])
        for half in range(2):
            wait_bytes(conv.at[half, part], csend_sem.at[half, part])


def local(inner_gate, values, outer_gate, filters, skip_gain, w_out):
    f32, bf16 = jnp.float32, jnp.bfloat16
    dma = pltpu.SemaphoreType.DMA
    return pl.pallas_call(
        kernel,
        out_shape=jax.ShapeDtypeStruct((FINE, 512), bf16),
        in_specs=[pl.BlockSpec(memory_space=pl.ANY)] * 9,
        out_specs=pl.BlockSpec(memory_space=pltpu.VMEM),
        scratch_shapes=[
            pltpu.VMEM((FINE, 1024), bf16),
            pltpu.VMEM((FINE, 1024), bf16),
            pltpu.VMEM((FINE, 1024), bf16),
            pltpu.VMEM((FINE, 1024), f32),
            pltpu.VMEM((1, 1024), f32),
            pltpu.VMEM((1024, 4096), bf16),
            pltpu.VMEM((2 * FINE, 2 * FINE), bf16),
            pltpu.VMEM((2 * FINE, 2 * FINE), bf16),
            pltpu.VMEM((BINS, 4, FINE), f32),
            pltpu.VMEM((2, SEQ, 2, PART, FINE), bf16),
            pltpu.VMEM((2, SEQ, 2, PART, FINE), bf16),
            pltpu.VMEM((BINS, 2, PART, 2 * FINE), bf16),
            pltpu.VMEM((BINS, PART, 2 * FINE), f32),
            pltpu.VMEM((2, 2, SEQ, PART, 128), bf16),
            pltpu.VMEM((2, 2, SEQ, PART, 128), bf16),
            pltpu.VMEM((FINE, 1024), bf16),
            pltpu.VMEM((FINE, FINE), bf16),
            pltpu.VMEM((4, 4, 64, 1024), bf16),
            pltpu.VMEM((4, 4, 64, 1024), bf16),
            pltpu.VMEM((4, 64, 512), f32),
            pltpu.VMEM((4, 64, 512), bf16),
            pltpu.VMEM((4, 64, 512), bf16),
            dma((9,)),
            dma((2,)),
            dma((2,)),
            dma((2, 2)),
            dma((2, 2)),
            dma((4, 4)),
            dma((4, 4)),
            dma((4,)),
            dma((4,)),
        ],
        compiler_params=pltpu.CompilerParams(collective_id=0, has_side_effects=True, vmem_limit_bytes=56 * 2**20),
        name="hyena",
    )(inner_gate, values, outer_gate, filters, skip_gain.reshape(1, -1), w_out, *tables())


def solution(mesh):
    in_specs = (P("seq", "tp"), P("seq", "tp"), P("seq", "tp"), P("seq", "tp"), P("tp"), P("tp", None))
    return jax.shard_map(local, mesh=mesh, in_specs=in_specs, out_specs=P("seq", "tp"), check_vma=False)
```

```python
import math

import jax
import jax.numpy as jnp
import numpy as np
from jax import lax
from jax.experimental import pallas as pl
from jax.experimental.pallas import tpu as pltpu
from jax.sharding import PartitionSpec as P

MESH = pl.DeviceIdType.MESH
NT = (((1,), (1,)), ((), ()))
SEQ = 32
PART = 16
FINE = 256
BINS = 33
LENGTH = 2 * SEQ * FINE
CHUNKS = ((0, 64), (64, 64), (128, 64), (192, 32), (224, 32))


def twist(z, angle):
    c, s = math.cos(angle), math.sin(angle)
    re, im = z
    if abs(s) < 1e-9:
        return (re, im) if c > 0 else (-re, -im)
    if abs(c) < 1e-9:
        return (-im, re) if s > 0 else (im, -re)
    if abs(abs(c) - abs(s)) < 1e-9:
        a = abs(c)
        d, e = (re - im) * a, (re + im) * a
        if c > 0:
            return (d, e) if s > 0 else (e, -d)
        return (-e, d) if s > 0 else (-d, -e)
    return (re * c - im * s, re * s + im * c)


def cadd(a, b):
    return (a[0] + b[0], a[1] + b[1])


def csub(a, b):
    return (a[0] - b[0], a[1] - b[1])


def complex_dft(z, sign):
    n = len(z)
    if n == 1:
        return z
    even, odd = complex_dft(z[0::2], sign), complex_dft(z[1::2], sign)
    first, second = [], []
    for k in range(n // 2):
        t = twist(odd[k], sign * 2 * math.pi * k / n)
        first.append(cadd(even[k], t))
        second.append(csub(even[k], t))
    return first + second


def odd_bins(v):
    n = 2 * len(v)
    q = n // 4
    z = [twist((v[p], -v[p + q]), -2 * math.pi * p / n) for p in range(q)]
    bins = {}
    for r, value in enumerate(complex_dft(z, -1)):
        k = 4 * r + 1
        bins[k if k <= n // 2 else n - k] = value if k <= n // 2 else (value[0], -value[1])
    return bins


def real_dft(x):
    n = len(x)
    if n == 2:
        return {0: (x[0] + x[1], None), 1: (x[0] - x[1], None)}
    h = n // 2
    bins = {2 * k: value for k, value in real_dft([x[p] + x[p + h] for p in range(h)]).items()}
    bins.update(odd_bins([x[p] - x[p + h] for p in range(h)]))
    return bins


def padded_real_dft(x):
    bins = {2 * k: value for k, value in real_dft(x).items()}
    bins.update(odd_bins(x))
    return bins


def odd_back(bins, n):
    q = n // 4
    z = []
    for r in range(q):
        k = 4 * r + 1
        z.append(bins[k] if k <= n // 2 else (bins[n - k][0], -bins[n - k][1]))
    d = [twist(c, 2 * math.pi * p / n) for p, c in enumerate(complex_dft(z, 1))]
    return [a for a, _ in d] + [-b for _, b in d]


def real_back(bins, n):
    if n == 2:
        return [bins[0][0] + bins[1][0], bins[0][0] - bins[1][0]]
    u = real_back({k // 2: value for k, value in bins.items() if k % 2 == 0}, n // 2)
    v = odd_back(bins, n)
    return [a + b for a, b in zip(u, v)] + [a - b for a, b in zip(u, v)]


def half_real_back(bins, n):
    u = real_back({k // 2: value for k, value in bins.items() if k % 2 == 0}, n // 2)
    return [a + b for a, b in zip(u, odd_back(bins, n))]


def tables():
    idx = np.arange(FINE)
    ang = 2 * np.pi * ((idx[:, None] * idx[None, :]) % FINE) / FINE
    c, s = np.cos(ang), np.sin(ang)
    forward = np.block([[c, -s], [s, c]])
    back = np.block([[c, s], [-s, c]])
    tw = 2 * np.pi * np.arange(BINS)[:, None] * idx[None, :] / LENGTH
    scale = np.full((BINS, 1), 2.0 / LENGTH)
    scale[0] = scale[-1] = 1.0 / LENGTH
    twiddle = np.stack([np.cos(tw), np.sin(tw), np.cos(tw) * scale, np.sin(tw) * scale], 1)
    return (
        jnp.asarray(forward, jnp.bfloat16),
        jnp.asarray(back, jnp.bfloat16),
        jnp.asarray(twiddle, jnp.float32),
    )


def identity():
    row = lax.broadcasted_iota(jnp.int32, (FINE, FINE), 0)
    col = lax.broadcasted_iota(jnp.int32, (FINE, FINE), 1)
    return jnp.where(row == col, 1.0, 0.0).astype(jnp.bfloat16)


def transform(part, recv, forward, back, twiddle, spec, waves, conv):
    f32 = jnp.float32
    bf16 = jnp.bfloat16
    for kind in range(2):
        for lane in range(2):
            lanes = slice(lane * 128, lane * 128 + 128)
            bins = padded_real_dft([recv[part, p, kind, :, lanes].astype(f32) for p in range(SEQ)])
            for k, (re, im) in bins.items():
                c, s = twiddle[k, 0:1, lanes], twiddle[k, 1:2, lanes]
                if im is None:
                    a, b = re * c, -(re * s)
                else:
                    a, b = re * c + im * s, im * c - re * s
                spec[k, kind, :, lanes] = a.astype(bf16)
                spec[k, kind, :, lane * 128 + FINE : lane * 128 + FINE + 128] = b.astype(bf16)

    group = 11

    @pl.loop(0, BINS // group)
    def _(step):
        at = pl.ds(step * group, group)
        both = jnp.dot(
            spec[at].reshape(group * 2 * PART, 2 * FINE), forward[...], preferred_element_type=f32
        ).reshape(group, 2, PART, 2 * FINE)
        zr, zi = both[:, 0, :, :FINE], both[:, 0, :, FINE:]
        hr, hi = both[:, 1, :, :FINE], both[:, 1, :, FINE:]
        y = jnp.concatenate([zr * hr - zi * hi, zr * hi + zi * hr], axis=-1).astype(bf16)
        waves[at] = jnp.dot(y.reshape(group * PART, 2 * FINE), back[...], preferred_element_type=f32).reshape(
            group, PART, 2 * FINE
        )

    for lane in range(2):
        lanes = slice(lane * 128, lane * 128 + 128)
        bins = {}
        for k in range(BINS):
            re, im = waves[k, :, lanes], waves[k, :, lane * 128 + FINE : lane * 128 + FINE + 128]
            c, s = twiddle[k, 2:3, lanes], twiddle[k, 3:4, lanes]
            bins[k] = (re * c - im * s, None if k in (0, BINS - 1) else im * c + re * s)
        for p, y in enumerate(half_real_back(bins, 2 * SEQ)):
            conv[lane, part, p] = y.astype(bf16)


def kernel(
    inner_hbm, values_hbm, outer_hbm, filters_hbm, skip_hbm, w_hbm, forward_hbm, back_hbm, twiddle_hbm, out,
    inner, values, outer, filters, skip, w, forward, back, twiddle,
    send, recv, spec, waves, conv, turned, mixed, eye, psend, passed, precv, kept, zsend, zrecv,
    load_sem, send_sem, recv_sem, csend_sem, crecv_sem, rsend_sem, rrecv_sem, psend_sem, precv_sem, zsend_sem, zrecv_sem,
):
    f32 = jnp.float32
    bf16 = jnp.bfloat16
    me, tp = lax.axis_index("seq"), lax.axis_index("tp")
    y, z = tp // 2, lax.rem(tp, 2)
    loads = [
        pltpu.make_async_copy(a, b, load_sem.at[i])
        for i, (a, b) in enumerate((
            (inner_hbm, inner), (values_hbm, values), (filters_hbm, filters), (forward_hbm, forward), (back_hbm, back),
            (twiddle_hbm, twiddle), (outer_hbm, outer), (skip_hbm, skip), (w_hbm, w),
        ))
    ]
    for load in loads:
        load.start()
    barrier = pltpu.get_barrier_semaphore()

    @pl.loop(1, SEQ)
    def _(i):
        pl.semaphore_signal(barrier, inc=1, device_id={"seq": me ^ i}, device_id_type=MESH)

    for d in (1, 3):
        pl.semaphore_signal(barrier, inc=1, device_id={"tp": lax.rem(y + d, 4) * 2 + z}, device_id_type=MESH)
    pl.semaphore_signal(barrier, inc=1, device_id={"tp": y * 2 + 1 - z}, device_id_type=MESH)
    row = lax.broadcasted_iota(jnp.int32, (FINE, FINE), 0)
    col = lax.broadcasted_iota(jnp.int32, (FINE, FINE), 1)
    eye[...] = jnp.where(row == col, 1.0, 0.0).astype(bf16)
    for load in loads[:3]:
        load.wait()

    def spread(part, block):
        @pl.loop(0, 8)
        def _(i):
            peer = block * 8 + (lax.rem(me, 8) ^ (7 - i))

            @pl.when(peer != me)
            def _():
                pltpu.make_async_remote_copy(
                    send.at[part, peer], recv.at[part, me], send_sem.at[part], recv_sem.at[part],
                    device_id={"seq": peer}, device_id_type=MESH,
                ).start()

    def pack(block):
        cols = pl.ds(pl.multiple_of(block * FINE, FINE), FINE)
        product = (inner[:, cols].astype(f32) * values[:, cols].astype(f32)).astype(bf16)
        for kind, piece in enumerate((product, filters[:, cols].astype(bf16))):
            flat = lax.dot_general(eye[...], piece, NT, preferred_element_type=f32).astype(bf16).reshape(8, 2, PART, FINE)
            for part in range(2):
                send[part, pl.ds(block * 8, 8), kind] = flat[:, part]

    first = lax.rem(me // 8 + 1, 4)
    pack(first)
    pl.semaphore_wait(barrier, SEQ + 2)
    spread(0, first)

    @pl.loop(1, 4)
    def _(step):
        block = lax.rem(me // 8 + 1 + step, 4)
        pack(block)
        spread(0, block)

    @pl.loop(0, 4)
    def _(step):
        spread(1, lax.rem(me // 8 + 1 + step, 4))

    for part in range(2):
        recv[part, me] = send[part, me]
    for load in loads[3:6]:
        load.wait()

    def give_back(half, part):
        @pl.loop(1, SEQ)
        def _(i):
            peer = me ^ (SEQ - i)
            pltpu.make_async_remote_copy(
                conv.at[half, part, peer], turned.at[half, part, me], csend_sem.at[half, part], crecv_sem.at[half, part],
                device_id={"seq": peer}, device_id_type=MESH,
            ).start()

        turned[half, part, me] = conv[half, part, me]

    def wait_bytes(ref, sem):
        pltpu.make_async_copy(ref.at[pl.ds(0, SEQ - 1)], ref.at[pl.ds(0, SEQ - 1)], sem).wait()

    @pl.loop(0, 2)
    def _(part):
        wait_bytes(recv.at[part], recv_sem.at[part])

        @pl.when(part == 1)
        def _():
            give_back(0, 0)

        transform(part, recv, forward, back, twiddle, spec, waves, conv)

    give_back(0, 1)
    give_back(1, 0)
    give_back(1, 1)
    for load in loads[6:]:
        load.wait()

    def mix(half):
        for part in range(2):
            wait_bytes(turned.at[half, part], crecv_sem.at[half, part])
        rows = slice(half * 128, half * 128 + 128)

        @pl.loop(0, 4)
        def _(block):
            cols = pl.ds(pl.multiple_of(block * FINE, FINE), FINE)
            both = [turned[half, part, pl.ds(block * 8, 8)].reshape(8, 1, PART, 128) for part in range(2)]
            piece = jnp.concatenate(both, axis=1).reshape(FINE, 128)
            here = lax.dot_general(eye[:128, :128], piece, NT, preferred_element_type=f32)
            product = inner[rows, cols].astype(f32) * values[rows, cols].astype(f32)
            mixed[rows, cols] = (outer[rows, cols].astype(f32) * (here + skip[:, cols] * product)).astype(bf16)

    def beside(step):
        return {"tp": lax.rem(y + 1 + 2 * step, 4) * 2 + z}

    def relay(chunk, step):
        rows = pl.ds(0, CHUNKS[chunk][1])
        return pltpu.make_async_remote_copy(
            psend.at[chunk, 2, step, rows], passed.at[chunk, step, rows], rsend_sem.at[chunk, step], rrecv_sem.at[chunk, step],
            device_id=beside(step), device_id_type=MESH,
        )

    def share(chunk, step, piece):
        rows = pl.ds(0, CHUNKS[chunk][1])
        return pltpu.make_async_remote_copy(
            psend.at[chunk, 1 + 2 * step, piece, rows], precv.at[chunk, step, piece, rows],
            psend_sem.at[chunk, step, piece], precv_sem.at[chunk, step, piece],
            device_id=beside(step), device_id_type=MESH,
        )

    def swap(chunk):
        rows = pl.ds(0, CHUNKS[chunk][1])
        return pltpu.make_async_remote_copy(
            zsend.at[chunk, rows], zrecv.at[chunk, rows], zsend_sem.at[chunk], zrecv_sem.at[chunk],
            device_id={"tp": y * 2 + 1 - z}, device_id_type=MESH,
        )

    def produce(chunk):
        start, count = CHUNKS[chunk]
        for d in (2, 1, 3, 0):
            target = lax.rem(y + d, 4)

            @pl.loop(0, 2)
            def _(piece):
                cols = pl.ds(pl.multiple_of(target * 1024 + piece * 512, 512), 512)
                psend[chunk, d, piece, 0:count] = jnp.dot(
                    mixed[start : start + count, :], w[:, cols], preferred_element_type=f32
                ).astype(bf16)

            if d == 2:
                relay(chunk, 0).start()
                relay(chunk, 1).start()
            elif d:
                share(chunk, d // 2, 1 - d // 2).start()

    def forward_on(chunk):
        count = CHUNKS[chunk][1]
        for step in range(2):
            relay(chunk, step).wait_recv()
            both = psend[chunk, 1 + 2 * step, step, 0:count].astype(f32) + passed[chunk, step, 0:count].astype(f32)
            psend[chunk, 1 + 2 * step, step, 0:count] = both.astype(bf16)
            share(chunk, step, step).start()

    def add_up(chunk):
        count = CHUNKS[chunk][1]
        for step in range(2):
            for piece in range(2):
                share(chunk, step, piece).wait_recv()

        def total(piece):
            acc = psend[chunk, 0, piece, 0:count].astype(f32)
            for step in range(2):
                acc += precv[chunk, step, piece, 0:count].astype(f32)
            return acc

        zsend[chunk, 0:count] = total(1 - z).astype(bf16)
        swap(chunk).start()
        kept[chunk, 0:count] = total(z)

    def finish(chunk):
        start, count = CHUNKS[chunk]
        swap(chunk).wait()
        out[start : start + count, :] = (kept[chunk, 0:count] + zrecv[chunk, 0:count].astype(f32)).astype(bf16)

    mix(0)
    produce(0)
    produce(1)
    forward_on(0)
    forward_on(1)
    mix(1)
    produce(2)
    add_up(0)
    produce(3)
    forward_on(2)
    add_up(1)
    produce(4)
    forward_on(3)
    add_up(2)
    forward_on(4)
    finish(0)
    add_up(3)
    finish(1)
    add_up(4)
    for chunk in range(2, 5):
        finish(chunk)
    for chunk in range(5):
        for step in range(2):
            relay(chunk, step).wait_send()
            for piece in range(2):
                share(chunk, step, piece).wait_send()
    for part in range(2):
        wait_bytes(send.at[part], send_sem.at[part])
        for half in range(2):
            wait_bytes(conv.at[half, part], csend_sem.at[half, part])


def local(inner_gate, values, outer_gate, filters, skip_gain, w_out):
    f32, bf16 = jnp.float32, jnp.bfloat16
    dma = pltpu.SemaphoreType.DMA
    return pl.pallas_call(
        kernel,
        out_shape=jax.ShapeDtypeStruct((FINE, 512), bf16),
        in_specs=[pl.BlockSpec(memory_space=pl.ANY)] * 9,
        out_specs=pl.BlockSpec(memory_space=pltpu.VMEM),
        scratch_shapes=[
            pltpu.VMEM((FINE, 1024), bf16),
            pltpu.VMEM((FINE, 1024), bf16),
            pltpu.VMEM((FINE, 1024), bf16),
            pltpu.VMEM((FINE, 1024), f32),
            pltpu.VMEM((1, 1024), f32),
            pltpu.VMEM((1024, 4096), bf16),
            pltpu.VMEM((2 * FINE, 2 * FINE), bf16),
            pltpu.VMEM((2 * FINE, 2 * FINE), bf16),
            pltpu.VMEM((BINS, 4, FINE), f32),
            pltpu.VMEM((2, SEQ, 2, PART, FINE), bf16),
            pltpu.VMEM((2, SEQ, 2, PART, FINE), bf16),
            pltpu.VMEM((BINS, 2, PART, 2 * FINE), bf16),
            pltpu.VMEM((BINS, PART, 2 * FINE), f32),
            pltpu.VMEM((2, 2, SEQ, PART, 128), bf16),
            pltpu.VMEM((2, 2, SEQ, PART, 128), bf16),
            pltpu.VMEM((FINE, 1024), bf16),
            pltpu.VMEM((FINE, FINE), bf16),
            pltpu.VMEM((5, 4, 2, 64, 512), bf16),
            pltpu.VMEM((5, 2, 64, 512), bf16),
            pltpu.VMEM((5, 2, 2, 64, 512), bf16),
            pltpu.VMEM((5, 64, 512), f32),
            pltpu.VMEM((5, 64, 512), bf16),
            pltpu.VMEM((5, 64, 512), bf16),
            dma((9,)),
            dma((2,)),
            dma((2,)),
            dma((2, 2)),
            dma((2, 2)),
            dma((5, 2)),
            dma((5, 2)),
            dma((5, 2, 2)),
            dma((5, 2, 2)),
            dma((5,)),
            dma((5,)),
        ],
        compiler_params=pltpu.CompilerParams(collective_id=0, has_side_effects=True, vmem_limit_bytes=56 * 2**20),
        name="hyena",
    )(inner_gate, values, outer_gate, filters, skip_gain.reshape(1, -1), w_out, *tables())


def solution(mesh):
    in_specs = (P("seq", "tp"), P("seq", "tp"), P("seq", "tp"), P("seq", "tp"), P("tp"), P("tp", None))
    return jax.shard_map(local, mesh=mesh, in_specs=in_specs, out_specs=P("seq", "tp"), check_vma=False)
```

```python
import math

import jax
import jax.numpy as jnp
import numpy as np
from jax import lax
from jax.experimental import pallas as pl
from jax.experimental.pallas import tpu as pltpu
from jax.sharding import PartitionSpec as P

MESH = pl.DeviceIdType.MESH
NT = (((1,), (1,)), ((), ()))
SEQ = 32
PART = 16
FINE = 256
BINS = 33
LENGTH = 2 * SEQ * FINE
CHUNKS = ((0, 64), (64, 64), (128, 64), (192, 64))


def twist(z, angle):
    c, s = math.cos(angle), math.sin(angle)
    re, im = z
    if abs(s) < 1e-9:
        return (re, im) if c > 0 else (-re, -im)
    if abs(c) < 1e-9:
        return (-im, re) if s > 0 else (im, -re)
    if abs(abs(c) - abs(s)) < 1e-9:
        a = abs(c)
        d, e = (re - im) * a, (re + im) * a
        if c > 0:
            return (d, e) if s > 0 else (e, -d)
        return (-e, d) if s > 0 else (-d, -e)
    return (re * c - im * s, re * s + im * c)


def cadd(a, b):
    return (a[0] + b[0], a[1] + b[1])


def csub(a, b):
    return (a[0] - b[0], a[1] - b[1])


def complex_dft(z, sign):
    n = len(z)
    if n == 1:
        return z
    even, odd = complex_dft(z[0::2], sign), complex_dft(z[1::2], sign)
    first, second = [], []
    for k in range(n // 2):
        t = twist(odd[k], sign * 2 * math.pi * k / n)
        first.append(cadd(even[k], t))
        second.append(csub(even[k], t))
    return first + second


def odd_bins(v):
    n = 2 * len(v)
    q = n // 4
    z = [twist((v[p], -v[p + q]), -2 * math.pi * p / n) for p in range(q)]
    bins = {}
    for r, value in enumerate(complex_dft(z, -1)):
        k = 4 * r + 1
        bins[k if k <= n // 2 else n - k] = value if k <= n // 2 else (value[0], -value[1])
    return bins


def real_dft(x):
    n = len(x)
    if n == 2:
        return {0: (x[0] + x[1], None), 1: (x[0] - x[1], None)}
    h = n // 2
    bins = {2 * k: value for k, value in real_dft([x[p] + x[p + h] for p in range(h)]).items()}
    bins.update(odd_bins([x[p] - x[p + h] for p in range(h)]))
    return bins


def padded_real_dft(x):
    bins = {2 * k: value for k, value in real_dft(x).items()}
    bins.update(odd_bins(x))
    return bins


def odd_back(bins, n):
    q = n // 4
    z = []
    for r in range(q):
        k = 4 * r + 1
        z.append(bins[k] if k <= n // 2 else (bins[n - k][0], -bins[n - k][1]))
    d = [twist(c, 2 * math.pi * p / n) for p, c in enumerate(complex_dft(z, 1))]
    return [a for a, _ in d] + [-b for _, b in d]


def real_back(bins, n):
    if n == 2:
        return [bins[0][0] + bins[1][0], bins[0][0] - bins[1][0]]
    u = real_back({k // 2: value for k, value in bins.items() if k % 2 == 0}, n // 2)
    v = odd_back(bins, n)
    return [a + b for a, b in zip(u, v)] + [a - b for a, b in zip(u, v)]


def half_real_back(bins, n):
    u = real_back({k // 2: value for k, value in bins.items() if k % 2 == 0}, n // 2)
    return [a + b for a, b in zip(u, odd_back(bins, n))]


def tables():
    idx = np.arange(FINE)
    ang = 2 * np.pi * ((idx[:, None] * idx[None, :]) % FINE) / FINE
    c, s = np.cos(ang), np.sin(ang)
    forward = np.block([[c, -s], [s, c]])
    back = np.block([[c, s], [-s, c]])
    tw = 2 * np.pi * np.arange(BINS)[:, None] * idx[None, :] / LENGTH
    scale = np.full((BINS, 1), 2.0 / LENGTH)
    scale[0] = scale[-1] = 1.0 / LENGTH
    twiddle = np.stack([np.cos(tw), np.sin(tw), np.cos(tw) * scale, np.sin(tw) * scale], 1)
    return (
        jnp.asarray(forward, jnp.bfloat16),
        jnp.asarray(back, jnp.bfloat16),
        jnp.asarray(twiddle, jnp.float32),
    )


def identity():
    row = lax.broadcasted_iota(jnp.int32, (FINE, FINE), 0)
    col = lax.broadcasted_iota(jnp.int32, (FINE, FINE), 1)
    return jnp.where(row == col, 1.0, 0.0).astype(jnp.bfloat16)


def transform(part, recv, forward, back, twiddle, spec, waves, conv):
    f32 = jnp.float32
    bf16 = jnp.bfloat16
    for kind in range(2):
        for lane in range(2):
            lanes = slice(lane * 128, lane * 128 + 128)
            bins = padded_real_dft([recv[part, p, kind, :, lanes].astype(f32) for p in range(SEQ)])
            for k, (re, im) in bins.items():
                c, s = twiddle[k, 0:1, lanes], twiddle[k, 1:2, lanes]
                if im is None:
                    a, b = re * c, -(re * s)
                else:
                    a, b = re * c + im * s, im * c - re * s
                spec[k, kind, :, lanes] = a.astype(bf16)
                spec[k, kind, :, lane * 128 + FINE : lane * 128 + FINE + 128] = b.astype(bf16)

    group = 33

    @pl.loop(0, BINS // group)
    def _(step):
        at = pl.ds(step * group, group)
        both = jnp.dot(
            spec[at].reshape(group * 2 * PART, 2 * FINE), forward[...], preferred_element_type=f32
        ).reshape(group, 2, PART, 2 * FINE)
        zr, zi = both[:, 0, :, :FINE], both[:, 0, :, FINE:]
        hr, hi = both[:, 1, :, :FINE], both[:, 1, :, FINE:]
        y = jnp.concatenate([zr * hr - zi * hi, zr * hi + zi * hr], axis=-1).astype(bf16)
        waves[at] = jnp.dot(y.reshape(group * PART, 2 * FINE), back[...], preferred_element_type=f32).reshape(
            group, PART, 2 * FINE
        )

    for lane in range(2):
        lanes = slice(lane * 128, lane * 128 + 128)
        bins = {}
        for k in range(BINS):
            re, im = waves[k, :, lanes], waves[k, :, lane * 128 + FINE : lane * 128 + FINE + 128]
            c, s = twiddle[k, 2:3, lanes], twiddle[k, 3:4, lanes]
            bins[k] = (re * c - im * s, None if k in (0, BINS - 1) else im * c + re * s)
        for p, y in enumerate(half_real_back(bins, 2 * SEQ)):
            conv[lane, part, p] = y.astype(bf16)


def kernel(
    inner_hbm, values_hbm, outer_hbm, filters_hbm, skip_hbm, w_hbm, forward_hbm, back_hbm, twiddle_hbm, out,
    inner, values, outer, filters, skip, w, forward, back, twiddle,
    send, recv, spec, waves, conv, turned, mixed, eye, psend, passed, precv, kept, zsend, zrecv,
    load_sem, send_sem, recv_sem, csend_sem, crecv_sem, rsend_sem, rrecv_sem, psend_sem, precv_sem, zsend_sem, zrecv_sem,
):
    f32 = jnp.float32
    bf16 = jnp.bfloat16
    me, tp = lax.axis_index("seq"), lax.axis_index("tp")
    y, z = tp // 2, lax.rem(tp, 2)
    loads = [
        pltpu.make_async_copy(a, b, load_sem.at[i])
        for i, (a, b) in enumerate((
            (inner_hbm, inner), (values_hbm, values), (filters_hbm, filters), (forward_hbm, forward), (back_hbm, back),
            (twiddle_hbm, twiddle), (outer_hbm, outer), (skip_hbm, skip), (w_hbm, w),
        ))
    ]
    for load in loads:
        load.start()
    barrier = pltpu.get_barrier_semaphore()

    @pl.loop(1, SEQ)
    def _(i):
        pl.semaphore_signal(barrier, inc=1, device_id={"seq": me ^ i}, device_id_type=MESH)

    for d in (1, 3):
        pl.semaphore_signal(barrier, inc=1, device_id={"tp": lax.rem(y + d, 4) * 2 + z}, device_id_type=MESH)
    pl.semaphore_signal(barrier, inc=1, device_id={"tp": y * 2 + 1 - z}, device_id_type=MESH)
    row = lax.broadcasted_iota(jnp.int32, (FINE, FINE), 0)
    col = lax.broadcasted_iota(jnp.int32, (FINE, FINE), 1)
    eye[...] = jnp.where(row == col, 1.0, 0.0).astype(bf16)
    for load in loads[:3]:
        load.wait()

    def spread(part, block):
        @pl.loop(0, 8)
        def _(i):
            peer = block * 8 + (lax.rem(me, 8) ^ (7 - i))

            @pl.when(peer != me)
            def _():
                pltpu.make_async_remote_copy(
                    send.at[part, peer], recv.at[part, me], send_sem.at[part], recv_sem.at[part],
                    device_id={"seq": peer}, device_id_type=MESH,
                ).start()

    def pack(block):
        cols = pl.ds(pl.multiple_of(block * FINE, FINE), FINE)
        product = (inner[:, cols].astype(f32) * values[:, cols].astype(f32)).astype(bf16)
        for kind, piece in enumerate((product, filters[:, cols].astype(bf16))):
            flat = lax.dot_general(eye[...], piece, NT, preferred_element_type=f32).astype(bf16).reshape(8, 2, PART, FINE)
            for part in range(2):
                send[part, pl.ds(block * 8, 8), kind] = flat[:, part]

    first = lax.rem(me // 8 + 1, 4)
    pack(first)
    pl.semaphore_wait(barrier, SEQ + 2)
    spread(0, first)

    @pl.loop(1, 4)
    def _(step):
        block = lax.rem(me // 8 + 1 + step, 4)
        pack(block)
        spread(0, block)

    @pl.loop(0, 4)
    def _(step):
        spread(1, lax.rem(me // 8 + 1 + step, 4))

    for part in range(2):
        recv[part, me] = send[part, me]
    for load in loads[3:6]:
        load.wait()

    def give_back(half, part):
        @pl.loop(1, SEQ)
        def _(i):
            peer = me ^ (SEQ - i)
            pltpu.make_async_remote_copy(
                conv.at[half, part, peer], turned.at[half, part, me], csend_sem.at[half, part], crecv_sem.at[half, part],
                device_id={"seq": peer}, device_id_type=MESH,
            ).start()

        turned[half, part, me] = conv[half, part, me]

    def wait_bytes(ref, sem):
        pltpu.make_async_copy(ref.at[pl.ds(0, SEQ - 1)], ref.at[pl.ds(0, SEQ - 1)], sem).wait()

    @pl.loop(0, 2)
    def _(part):
        wait_bytes(recv.at[part], recv_sem.at[part])

        @pl.when(part == 1)
        def _():
            give_back(0, 0)

        transform(part, recv, forward, back, twiddle, spec, waves, conv)

    give_back(0, 1)
    give_back(1, 0)
    give_back(1, 1)
    for load in loads[6:]:
        load.wait()

    def mix(half):
        for part in range(2):
            wait_bytes(turned.at[half, part], crecv_sem.at[half, part])
        rows = slice(half * 128, half * 128 + 128)

        @pl.loop(0, 4)
        def _(block):
            cols = pl.ds(pl.multiple_of(block * FINE, FINE), FINE)
            both = [turned[half, part, pl.ds(block * 8, 8)].reshape(8, 1, PART, 128) for part in range(2)]
            piece = jnp.concatenate(both, axis=1).reshape(FINE, 128)
            here = lax.dot_general(eye[:128, :128], piece, NT, preferred_element_type=f32)
            product = inner[rows, cols].astype(f32) * values[rows, cols].astype(f32)
            mixed[rows, cols] = (outer[rows, cols].astype(f32) * (here + skip[:, cols] * product)).astype(bf16)

    def beside(step):
        return {"tp": lax.rem(y + 1 + 2 * step, 4) * 2 + z}

    def relay(chunk, step):
        rows = pl.ds(0, CHUNKS[chunk][1])
        return pltpu.make_async_remote_copy(
            psend.at[chunk, 2, step, rows], passed.at[chunk, step, rows], rsend_sem.at[chunk, step], rrecv_sem.at[chunk, step],
            device_id=beside(step), device_id_type=MESH,
        )

    def share(chunk, step, piece):
        rows = pl.ds(0, CHUNKS[chunk][1])
        return pltpu.make_async_remote_copy(
            psend.at[chunk, 1 + 2 * step, piece, rows], precv.at[chunk, step, piece, rows],
            psend_sem.at[chunk, step, piece], precv_sem.at[chunk, step, piece],
            device_id=beside(step), device_id_type=MESH,
        )

    def swap(chunk):
        rows = pl.ds(0, CHUNKS[chunk][1])
        return pltpu.make_async_remote_copy(
            zsend.at[chunk, rows], zrecv.at[chunk, rows], zsend_sem.at[chunk], zrecv_sem.at[chunk],
            device_id={"tp": y * 2 + 1 - z}, device_id_type=MESH,
        )

    def produce(half):
        chunks = [c for c, (start, _) in enumerate(CHUNKS) if start // 128 == half]
        for d in (2, 1, 3, 0):
            target = lax.rem(y + d, 4)

            @pl.loop(0, 2)
            def _(piece):
                cols = pl.ds(pl.multiple_of(target * 1024 + piece * 512, 512), 512)
                part = jnp.dot(
                    mixed[half * 128 : half * 128 + 128, :], w[:, cols], preferred_element_type=f32
                ).astype(bf16)
                for c in chunks:
                    start, count = CHUNKS[c]
                    psend[c, d, piece, 0:count] = part[start - half * 128 : start - half * 128 + count]

            for c in chunks:
                if d == 2:
                    relay(c, 0).start()
                    relay(c, 1).start()
                elif d:
                    share(c, d // 2, 1 - d // 2).start()

    def forward_on(chunk):
        count = CHUNKS[chunk][1]
        for step in range(2):
            relay(chunk, step).wait_recv()
            both = psend[chunk, 1 + 2 * step, step, 0:count].astype(f32) + passed[chunk, step, 0:count].astype(f32)
            psend[chunk, 1 + 2 * step, step, 0:count] = both.astype(bf16)
            share(chunk, step, step).start()

    def add_up(chunk):
        count = CHUNKS[chunk][1]
        for step in range(2):
            for piece in range(2):
                share(chunk, step, piece).wait_recv()

        def total(piece):
            acc = psend[chunk, 0, piece, 0:count].astype(f32)
            for step in range(2):
                acc += precv[chunk, step, piece, 0:count].astype(f32)
            return acc

        zsend[chunk, 0:count] = total(1 - z).astype(bf16)
        swap(chunk).start()
        kept[chunk, 0:count] = total(z)

    def finish(chunk):
        start, count = CHUNKS[chunk]
        swap(chunk).wait()
        out[start : start + count, :] = (kept[chunk, 0:count] + zrecv[chunk, 0:count].astype(f32)).astype(bf16)

    mix(0)
    produce(0)
    forward_on(0)
    forward_on(1)
    mix(1)
    produce(1)
    add_up(0)
    add_up(1)
    forward_on(2)
    forward_on(3)
    finish(0)
    add_up(2)
    finish(1)
    add_up(3)
    finish(2)
    finish(3)
    for chunk in range(len(CHUNKS)):
        for step in range(2):
            relay(chunk, step).wait_send()
            for piece in range(2):
                share(chunk, step, piece).wait_send()
    for part in range(2):
        wait_bytes(send.at[part], send_sem.at[part])
        for half in range(2):
            wait_bytes(conv.at[half, part], csend_sem.at[half, part])


def local(inner_gate, values, outer_gate, filters, skip_gain, w_out):
    f32, bf16 = jnp.float32, jnp.bfloat16
    dma = pltpu.SemaphoreType.DMA
    return pl.pallas_call(
        kernel,
        out_shape=jax.ShapeDtypeStruct((FINE, 512), bf16),
        in_specs=[pl.BlockSpec(memory_space=pl.ANY)] * 9,
        out_specs=pl.BlockSpec(memory_space=pltpu.VMEM),
        scratch_shapes=[
            pltpu.VMEM((FINE, 1024), bf16),
            pltpu.VMEM((FINE, 1024), bf16),
            pltpu.VMEM((FINE, 1024), bf16),
            pltpu.VMEM((FINE, 1024), f32),
            pltpu.VMEM((1, 1024), f32),
            pltpu.VMEM((1024, 4096), bf16),
            pltpu.VMEM((2 * FINE, 2 * FINE), bf16),
            pltpu.VMEM((2 * FINE, 2 * FINE), bf16),
            pltpu.VMEM((BINS, 4, FINE), f32),
            pltpu.VMEM((2, SEQ, 2, PART, FINE), bf16),
            pltpu.VMEM((2, SEQ, 2, PART, FINE), bf16),
            pltpu.VMEM((BINS, 2, PART, 2 * FINE), bf16),
            pltpu.VMEM((BINS, PART, 2 * FINE), f32),
            pltpu.VMEM((2, 2, SEQ, PART, 128), bf16),
            pltpu.VMEM((2, 2, SEQ, PART, 128), bf16),
            pltpu.VMEM((FINE, 1024), bf16),
            pltpu.VMEM((FINE, FINE), bf16),
            pltpu.VMEM((4, 4, 2, 64, 512), bf16),
            pltpu.VMEM((4, 2, 64, 512), bf16),
            pltpu.VMEM((4, 2, 2, 64, 512), bf16),
            pltpu.VMEM((4, 64, 512), f32),
            pltpu.VMEM((4, 64, 512), bf16),
            pltpu.VMEM((4, 64, 512), bf16),
            dma((9,)),
            dma((2,)),
            dma((2,)),
            dma((2, 2)),
            dma((2, 2)),
            dma((4, 2)),
            dma((4, 2)),
            dma((4, 2, 2)),
            dma((4, 2, 2)),
            dma((4,)),
            dma((4,)),
        ],
        compiler_params=pltpu.CompilerParams(collective_id=0, has_side_effects=True, vmem_limit_bytes=56 * 2**20),
        name="hyena",
    )(inner_gate, values, outer_gate, filters, skip_gain.reshape(1, -1), w_out, *tables())


def solution(mesh):
    in_specs = (P("seq", "tp"), P("seq", "tp"), P("seq", "tp"), P("seq", "tp"), P("tp"), P("tp", None))
    return jax.shard_map(local, mesh=mesh, in_specs=in_specs, out_specs=P("seq", "tp"), check_vma=False)
```

```python
import math

import jax
import jax.numpy as jnp
import numpy as np
from jax import lax
from jax.experimental import pallas as pl
from jax.experimental.pallas import tpu as pltpu
from jax.sharding import PartitionSpec as P

MESH = pl.DeviceIdType.MESH
NT = (((1,), (1,)), ((), ()))
SEQ = 32
PART = 16
FINE = 256
BINS = 33
LENGTH = 2 * SEQ * FINE
CHUNKS = ((0, 64), (64, 64), (128, 64), (192, 64))


def twist(z, angle):
    c, s = math.cos(angle), math.sin(angle)
    re, im = z
    if abs(s) < 1e-9:
        return (re, im) if c > 0 else (-re, -im)
    if abs(c) < 1e-9:
        return (-im, re) if s > 0 else (im, -re)
    if abs(abs(c) - abs(s)) < 1e-9:
        a = abs(c)
        d, e = (re - im) * a, (re + im) * a
        if c > 0:
            return (d, e) if s > 0 else (e, -d)
        return (-e, d) if s > 0 else (-d, -e)
    return (re * c - im * s, re * s + im * c)


def cadd(a, b):
    return (a[0] + b[0], a[1] + b[1])


def csub(a, b):
    return (a[0] - b[0], a[1] - b[1])


def complex_dft(z, sign):
    n = len(z)
    if n == 1:
        return z
    even, odd = complex_dft(z[0::2], sign), complex_dft(z[1::2], sign)
    first, second = [], []
    for k in range(n // 2):
        t = twist(odd[k], sign * 2 * math.pi * k / n)
        first.append(cadd(even[k], t))
        second.append(csub(even[k], t))
    return first + second


def odd_bins(v):
    n = 2 * len(v)
    q = n // 4
    z = [twist((v[p], -v[p + q]), -2 * math.pi * p / n) for p in range(q)]
    bins = {}
    for r, value in enumerate(complex_dft(z, -1)):
        k = 4 * r + 1
        bins[k if k <= n // 2 else n - k] = value if k <= n // 2 else (value[0], -value[1])
    return bins


def real_dft(x):
    n = len(x)
    if n == 2:
        return {0: (x[0] + x[1], None), 1: (x[0] - x[1], None)}
    h = n // 2
    bins = {2 * k: value for k, value in real_dft([x[p] + x[p + h] for p in range(h)]).items()}
    bins.update(odd_bins([x[p] - x[p + h] for p in range(h)]))
    return bins


def padded_real_dft(x):
    bins = {2 * k: value for k, value in real_dft(x).items()}
    bins.update(odd_bins(x))
    return bins


def odd_back(bins, n):
    q = n // 4
    z = []
    for r in range(q):
        k = 4 * r + 1
        z.append(bins[k] if k <= n // 2 else (bins[n - k][0], -bins[n - k][1]))
    d = [twist(c, 2 * math.pi * p / n) for p, c in enumerate(complex_dft(z, 1))]
    return [a for a, _ in d] + [-b for _, b in d]


def real_back(bins, n):
    if n == 2:
        return [bins[0][0] + bins[1][0], bins[0][0] - bins[1][0]]
    u = real_back({k // 2: value for k, value in bins.items() if k % 2 == 0}, n // 2)
    v = odd_back(bins, n)
    return [a + b for a, b in zip(u, v)] + [a - b for a, b in zip(u, v)]


def half_real_back(bins, n):
    u = real_back({k // 2: value for k, value in bins.items() if k % 2 == 0}, n // 2)
    return [a + b for a, b in zip(u, odd_back(bins, n))]


def tables():
    idx = np.arange(FINE)
    ang = 2 * np.pi * ((idx[:, None] * idx[None, :]) % FINE) / FINE
    c, s = np.cos(ang), np.sin(ang)
    forward = np.block([[c, -s], [s, c]])
    back = np.block([[c, s], [-s, c]])
    tw = 2 * np.pi * np.arange(BINS)[:, None] * idx[None, :] / LENGTH
    scale = np.full((BINS, 1), 2.0 / LENGTH)
    scale[0] = scale[-1] = 1.0 / LENGTH
    twiddle = np.stack([np.cos(tw), np.sin(tw), np.cos(tw) * scale, np.sin(tw) * scale], 1)
    return (
        jnp.asarray(forward, jnp.bfloat16),
        jnp.asarray(back, jnp.bfloat16),
        jnp.asarray(np.pad(twiddle, ((0, 2 * BINS), (0, 4), (0, 0))), jnp.float32),
    )


def identity():
    for load in loads:
        load.start()
    row = lax.broadcasted_iota(jnp.int32, (FINE, FINE), 0)
    col = lax.broadcasted_iota(jnp.int32, (FINE, FINE), 1)
    return jnp.where(row == col, 1.0, 0.0).astype(jnp.bfloat16)


def transform(part, recv, forward, back, twiddle, spec, waves, conv):
    f32 = jnp.float32
    bf16 = jnp.bfloat16
    for kind in range(2):
        for lane in range(2):
            lanes = slice(lane * 128, lane * 128 + 128)
            bins = padded_real_dft([recv[part, p, kind, :, lanes].astype(f32) for p in range(SEQ)])
            for k, (re, im) in bins.items():
                c, s = twiddle[k, 0:1, lanes], twiddle[k, 1:2, lanes]
                if im is None:
                    a, b = re * c, -(re * s)
                else:
                    a, b = re * c + im * s, im * c - re * s
                spec[k, kind, :, lanes] = a.astype(bf16)
                spec[k, kind, :, lane * 128 + FINE : lane * 128 + FINE + 128] = b.astype(bf16)

    group = 33

    @pl.loop(0, BINS // group)
    def _(step):
        at = pl.ds(step * group, group)
        both = jnp.dot(
            spec[at].reshape(group * 2 * PART, 2 * FINE), forward[...], preferred_element_type=f32
        ).reshape(group, 2, PART, 2 * FINE)
        zr, zi = both[:, 0, :, :FINE], both[:, 0, :, FINE:]
        hr, hi = both[:, 1, :, :FINE], both[:, 1, :, FINE:]
        y = jnp.concatenate([zr * hr - zi * hi, zr * hi + zi * hr], axis=-1).astype(bf16)
        waves[at] = jnp.dot(y.reshape(group * PART, 2 * FINE), back[...], preferred_element_type=f32).reshape(
            group, PART, 2 * FINE
        )

    for lane in range(2):
        lanes = slice(lane * 128, lane * 128 + 128)
        bins = {}
        for k in range(BINS):
            re, im = waves[k, :, lanes], waves[k, :, lane * 128 + FINE : lane * 128 + FINE + 128]
            c, s = twiddle[k, 2:3, lanes], twiddle[k, 3:4, lanes]
            bins[k] = (re * c - im * s, None if k in (0, BINS - 1) else im * c + re * s)
        for p, y in enumerate(half_real_back(bins, 2 * SEQ)):
            conv[lane, part, p] = y.astype(bf16)


def kernel(
    inner_hbm, values_hbm, outer_hbm, filters_hbm, skip_hbm, w_hbm, forward_hbm, back_hbm, twiddle_hbm, out,
    inner, values, outer, filters, skip, w, forward, back, twiddle,
    send, recv, spec, waves, conv, turned, mixed, eye, psend, passed, precv, kept, zsend, zrecv,
    load_sem, send_sem, recv_sem, csend_sem, crecv_sem, rsend_sem, rrecv_sem, psend_sem, precv_sem, zsend_sem, zrecv_sem,
):
    f32 = jnp.float32
    bf16 = jnp.bfloat16
    me, tp = lax.axis_index("seq"), lax.axis_index("tp")
    y, z = tp // 2, lax.rem(tp, 2)
    loads = [
        pltpu.make_async_copy(a, b, load_sem.at[i])
        for i, (a, b) in enumerate((
            (inner_hbm, inner), (values_hbm, values), (filters_hbm, filters), (forward_hbm, forward), (back_hbm, back),
            (twiddle_hbm.at[pl.ds(0, BINS)], twiddle), (outer_hbm, outer), (skip_hbm, skip), (w_hbm, w),
        ))
    ]
    barrier = pltpu.get_barrier_semaphore()

    @pl.loop(1, SEQ)
    def _(i):
        pl.semaphore_signal(barrier, inc=1, device_id={"seq": me ^ i}, device_id_type=MESH)

    for d in (1, 3):
        pl.semaphore_signal(barrier, inc=1, device_id={"tp": lax.rem(y + d, 4) * 2 + z}, device_id_type=MESH)
    pl.semaphore_signal(barrier, inc=1, device_id={"tp": y * 2 + 1 - z}, device_id_type=MESH)
    for load in loads:
        load.start()
    row = lax.broadcasted_iota(jnp.int32, (FINE, FINE), 0)
    col = lax.broadcasted_iota(jnp.int32, (FINE, FINE), 1)
    eye[...] = jnp.where(row == col, 1.0, 0.0).astype(bf16)
    for load in loads[:3]:
        load.wait()

    def spread(part, block):
        @pl.loop(0, 8)
        def _(i):
            peer = block * 8 + (lax.rem(me, 8) ^ (7 - i))

            @pl.when(peer != me)
            def _():
                pltpu.make_async_remote_copy(
                    send.at[part, peer], recv.at[part, me], send_sem.at[part], recv_sem.at[part],
                    device_id={"seq": peer}, device_id_type=MESH,
                ).start()

    def pack(block):
        cols = pl.ds(pl.multiple_of(block * FINE, FINE), FINE)
        product = (inner[:, cols].astype(f32) * values[:, cols].astype(f32)).astype(bf16)
        for kind, piece in enumerate((product, filters[:, cols].astype(bf16))):
            flat = lax.dot_general(eye[...], piece, NT, preferred_element_type=f32).astype(bf16).reshape(8, 2, PART, FINE)
            for part in range(2):
                send[part, pl.ds(block * 8, 8), kind] = flat[:, part]

    first = lax.rem(me // 8 + 1, 4)
    pack(first)
    pl.semaphore_wait(barrier, SEQ + 2)
    spread(0, first)

    @pl.loop(1, 4)
    def _(step):
        block = lax.rem(me // 8 + 1 + step, 4)
        pack(block)
        spread(0, block)

    @pl.loop(0, 4)
    def _(step):
        spread(1, lax.rem(me // 8 + 1 + step, 4))

    for part in range(2):
        recv[part, me] = send[part, me]
    for load in loads[3:6]:
        load.wait()

    def give_back(half, part):
        @pl.loop(1, SEQ)
        def _(i):
            peer = me ^ (SEQ - i)
            pltpu.make_async_remote_copy(
                conv.at[half, part, peer], turned.at[half, part, me], csend_sem.at[half, part], crecv_sem.at[half, part],
                device_id={"seq": peer}, device_id_type=MESH,
            ).start()

        turned[half, part, me] = conv[half, part, me]

    def wait_bytes(ref, sem):
        pltpu.make_async_copy(ref.at[pl.ds(0, SEQ - 1)], ref.at[pl.ds(0, SEQ - 1)], sem).wait()

    @pl.loop(0, 2)
    def _(part):
        wait_bytes(recv.at[part], recv_sem.at[part])

        @pl.when(part == 1)
        def _():
            give_back(0, 0)

        transform(part, recv, forward, back, twiddle, spec, waves, conv)

    give_back(0, 1)
    give_back(1, 0)
    give_back(1, 1)
    for load in loads[6:]:
        load.wait()

    def mix(half):
        for part in range(2):
            wait_bytes(turned.at[half, part], crecv_sem.at[half, part])
        rows = slice(half * 128, half * 128 + 128)

        @pl.loop(0, 4)
        def _(block):
            cols = pl.ds(pl.multiple_of(block * FINE, FINE), FINE)
            both = [turned[half, part, pl.ds(block * 8, 8)].reshape(8, 1, PART, 128) for part in range(2)]
            piece = jnp.concatenate(both, axis=1).reshape(FINE, 128)
            here = lax.dot_general(eye[:128, :128], piece, NT, preferred_element_type=f32)
            product = inner[rows, cols].astype(f32) * values[rows, cols].astype(f32)
            mixed[rows, cols] = (outer[rows, cols].astype(f32) * (here + skip[:, cols] * product)).astype(bf16)

    def beside(step):
        return {"tp": lax.rem(y + 1 + 2 * step, 4) * 2 + z}

    def relay(chunk, step):
        rows = pl.ds(0, CHUNKS[chunk][1])
        return pltpu.make_async_remote_copy(
            psend.at[chunk, 2, step, rows], passed.at[chunk, step, rows], rsend_sem.at[chunk, step], rrecv_sem.at[chunk, step],
            device_id=beside(step), device_id_type=MESH,
        )

    def share(chunk, step, piece):
        rows = pl.ds(0, CHUNKS[chunk][1])
        return pltpu.make_async_remote_copy(
            psend.at[chunk, 1 + 2 * step, piece, rows], precv.at[chunk, step, piece, rows],
            psend_sem.at[chunk, step, piece], precv_sem.at[chunk, step, piece],
            device_id=beside(step), device_id_type=MESH,
        )

    def swap(chunk):
        rows = pl.ds(0, CHUNKS[chunk][1])
        return pltpu.make_async_remote_copy(
            zsend.at[chunk, rows], zrecv.at[chunk, rows], zsend_sem.at[chunk], zrecv_sem.at[chunk],
            device_id={"tp": y * 2 + 1 - z}, device_id_type=MESH,
        )

    def produce(half):
        chunks = [c for c, (start, _) in enumerate(CHUNKS) if start // 128 == half]
        for d in (2, 1, 3, 0):
            target = lax.rem(y + d, 4)

            @pl.loop(0, 2)
            def _(piece):
                cols = pl.ds(pl.multiple_of(target * 1024 + piece * 512, 512), 512)
                part = jnp.dot(
                    mixed[half * 128 : half * 128 + 128, :], w[:, cols], preferred_element_type=f32
                ).astype(bf16)
                for c in chunks:
                    start, count = CHUNKS[c]
                    psend[c, d, piece, 0:count] = part[start - half * 128 : start - half * 128 + count]

            for c in chunks:
                if d == 2:
                    relay(c, 0).start()
                    relay(c, 1).start()
                elif d:
                    share(c, d // 2, 1 - d // 2).start()

    def forward_on(chunk):
        count = CHUNKS[chunk][1]
        for step in range(2):
            relay(chunk, step).wait_recv()
            both = psend[chunk, 1 + 2 * step, step, 0:count].astype(f32) + passed[chunk, step, 0:count].astype(f32)
            psend[chunk, 1 + 2 * step, step, 0:count] = both.astype(bf16)
            share(chunk, step, step).start()

    def add_up(chunk):
        count = CHUNKS[chunk][1]
        for step in range(2):
            for piece in range(2):
                share(chunk, step, piece).wait_recv()

        def total(piece):
            acc = psend[chunk, 0, piece, 0:count].astype(f32)
            for step in range(2):
                acc += precv[chunk, step, piece, 0:count].astype(f32)
            return acc

        zsend[chunk, 0:count] = total(1 - z).astype(bf16)
        swap(chunk).start()
        kept[chunk, 0:count] = total(z)

    def finish(chunk):
        start, count = CHUNKS[chunk]
        swap(chunk).wait()
        out[start : start + count, :] = (kept[chunk, 0:count] + zrecv[chunk, 0:count].astype(f32)).astype(bf16)

    mix(0)
    produce(0)
    forward_on(0)
    forward_on(1)
    mix(1)
    produce(1)
    add_up(0)
    add_up(1)
    forward_on(2)
    forward_on(3)
    finish(0)
    add_up(2)
    finish(1)
    add_up(3)
    finish(2)
    finish(3)
    for chunk in range(len(CHUNKS)):
        for step in range(2):
            relay(chunk, step).wait_send()
            for piece in range(2):
                share(chunk, step, piece).wait_send()
    for part in range(2):
        wait_bytes(send.at[part], send_sem.at[part])
        for half in range(2):
            wait_bytes(conv.at[half, part], csend_sem.at[half, part])


def local(inner_gate, values, outer_gate, filters, skip_gain, w_out):
    f32, bf16 = jnp.float32, jnp.bfloat16
    dma = pltpu.SemaphoreType.DMA
    return pl.pallas_call(
        kernel,
        out_shape=jax.ShapeDtypeStruct((FINE, 512), bf16),
        in_specs=[pl.BlockSpec(memory_space=pl.ANY)] * 9,
        out_specs=pl.BlockSpec(memory_space=pltpu.VMEM),
        scratch_shapes=[
            pltpu.VMEM((FINE, 1024), bf16),
            pltpu.VMEM((FINE, 1024), bf16),
            pltpu.VMEM((FINE, 1024), bf16),
            pltpu.VMEM((FINE, 1024), f32),
            pltpu.VMEM((1, 1024), f32),
            pltpu.VMEM((1024, 4096), bf16),
            pltpu.VMEM((2 * FINE, 2 * FINE), bf16),
            pltpu.VMEM((2 * FINE, 2 * FINE), bf16),
            pltpu.VMEM((BINS, 8, FINE), f32),
            pltpu.VMEM((2, SEQ, 2, PART, FINE), bf16),
            pltpu.VMEM((2, SEQ, 2, PART, FINE), bf16),
            pltpu.VMEM((BINS, 2, PART, 2 * FINE), bf16),
            pltpu.VMEM((BINS, PART, 2 * FINE), f32),
            pltpu.VMEM((2, 2, SEQ, PART, 128), bf16),
            pltpu.VMEM((2, 2, SEQ, PART, 128), bf16),
            pltpu.VMEM((FINE, 1024), bf16),
            pltpu.VMEM((FINE, FINE), bf16),
            pltpu.VMEM((4, 4, 2, 64, 512), bf16),
            pltpu.VMEM((4, 2, 64, 512), bf16),
            pltpu.VMEM((4, 2, 2, 64, 512), bf16),
            pltpu.VMEM((4, 64, 512), f32),
            pltpu.VMEM((4, 64, 512), bf16),
            pltpu.VMEM((4, 64, 512), bf16),
            dma((9,)),
            dma((2,)),
            dma((2,)),
            dma((2, 2)),
            dma((2, 2)),
            dma((4, 2)),
            dma((4, 2)),
            dma((4, 2, 2)),
            dma((4, 2, 2)),
            dma((4,)),
            dma((4,)),
        ],
        compiler_params=pltpu.CompilerParams(collective_id=0, has_side_effects=True, vmem_limit_bytes=56098816),
        name="hyena",
    )(inner_gate, values, outer_gate, filters, skip_gain.reshape(1, -1), w_out, *tables())


def solution(mesh):
    in_specs = (P("seq", "tp"), P("seq", "tp"), P("seq", "tp"), P("seq", "tp"), P("tp"), P("tp", None))
    return jax.shard_map(local, mesh=mesh, in_specs=in_specs, out_specs=P("seq", "tp"), check_vma=False)
```

```python
import math

import jax
import jax.numpy as jnp
import numpy as np
from jax import lax
from jax.experimental import pallas as pl
from jax.experimental.pallas import tpu as pltpu
from jax.sharding import PartitionSpec as P

MESH = pl.DeviceIdType.MESH
NT = (((1,), (1,)), ((), ()))
SEQ = 32
PART = 16
FINE = 256
BINS = 33
LENGTH = 2 * SEQ * FINE
CHUNKS = ((0, 64), (64, 64), (128, 64), (192, 64))


def twist(z, angle):
    c, s = math.cos(angle), math.sin(angle)
    re, im = z
    if abs(s) < 1e-9:
        return (re, im) if c > 0 else (-re, -im)
    if abs(c) < 1e-9:
        return (-im, re) if s > 0 else (im, -re)
    if abs(abs(c) - abs(s)) < 1e-9:
        a = abs(c)
        d, e = (re - im) * a, (re + im) * a
        if c > 0:
            return (d, e) if s > 0 else (e, -d)
        return (-e, d) if s > 0 else (-d, -e)
    return (re * c - im * s, re * s + im * c)


def cadd(a, b):
    return (a[0] + b[0], a[1] + b[1])


def csub(a, b):
    return (a[0] - b[0], a[1] - b[1])


def complex_dft(z, sign):
    n = len(z)
    if n == 1:
        return z
    even, odd = complex_dft(z[0::2], sign), complex_dft(z[1::2], sign)
    first, second = [], []
    for k in range(n // 2):
        t = twist(odd[k], sign * 2 * math.pi * k / n)
        first.append(cadd(even[k], t))
        second.append(csub(even[k], t))
    return first + second


def odd_bins(v):
    n = 2 * len(v)
    q = n // 4
    z = [twist((v[p], -v[p + q]), -2 * math.pi * p / n) for p in range(q)]
    bins = {}
    for r, value in enumerate(complex_dft(z, -1)):
        k = 4 * r + 1
        bins[k if k <= n // 2 else n - k] = value if k <= n // 2 else (value[0], -value[1])
    return bins


def real_dft(x):
    n = len(x)
    if n == 2:
        return {0: (x[0] + x[1], None), 1: (x[0] - x[1], None)}
    h = n // 2
    bins = {2 * k: value for k, value in real_dft([x[p] + x[p + h] for p in range(h)]).items()}
    bins.update(odd_bins([x[p] - x[p + h] for p in range(h)]))
    return bins


def padded_real_dft(x):
    bins = {2 * k: value for k, value in real_dft(x).items()}
    bins.update(odd_bins(x))
    return bins


def odd_back(bins, n):
    q = n // 4
    z = []
    for r in range(q):
        k = 4 * r + 1
        z.append(bins[k] if k <= n // 2 else (bins[n - k][0], -bins[n - k][1]))
    d = [twist(c, 2 * math.pi * p / n) for p, c in enumerate(complex_dft(z, 1))]
    return [a for a, _ in d] + [-b for _, b in d]


def real_back(bins, n):
    if n == 2:
        return [bins[0][0] + bins[1][0], bins[0][0] - bins[1][0]]
    u = real_back({k // 2: value for k, value in bins.items() if k % 2 == 0}, n // 2)
    v = odd_back(bins, n)
    return [a + b for a, b in zip(u, v)] + [a - b for a, b in zip(u, v)]


def half_real_back(bins, n):
    u = real_back({k // 2: value for k, value in bins.items() if k % 2 == 0}, n // 2)
    return [a + b for a, b in zip(u, odd_back(bins, n))]


def tables():
    idx = np.arange(FINE)
    ang = 2 * np.pi * ((idx[:, None] * idx[None, :]) % FINE) / FINE
    c, s = np.cos(ang), np.sin(ang)
    forward = np.block([[c, -s], [s, c]])
    back = np.block([[c, s], [-s, c]])
    tw = 2 * np.pi * np.arange(BINS)[:, None] * idx[None, :] / LENGTH
    scale = np.full((BINS, 1), 2.0 / LENGTH)
    scale[0] = scale[-1] = 1.0 / LENGTH
    twiddle = np.stack([np.cos(tw), np.sin(tw), np.cos(tw) * scale, np.sin(tw) * scale], 1)
    return (
        jnp.asarray(forward, jnp.bfloat16),
        jnp.asarray(back, jnp.bfloat16),
        jnp.asarray(np.pad(twiddle, ((0, 2 * BINS), (0, 4), (0, 0))), jnp.float32),
    )


def identity():
    for load in loads:
        load.start()
    row = lax.broadcasted_iota(jnp.int32, (FINE, FINE), 0)
    col = lax.broadcasted_iota(jnp.int32, (FINE, FINE), 1)
    return jnp.where(row == col, 1.0, 0.0).astype(jnp.bfloat16)


def transform(part, recv, forward, back, twiddle, spec, waves, conv):
    f32 = jnp.float32
    bf16 = jnp.bfloat16
    for kind in range(2):
        for lane in range(2):
            lanes = slice(lane * 128, lane * 128 + 128)
            bins = padded_real_dft([recv[part, p, kind, :, lanes].astype(f32) for p in range(SEQ)])
            for k, (re, im) in bins.items():
                c, s = twiddle[k, 0:1, lanes], twiddle[k, 1:2, lanes]
                if im is None:
                    a, b = re * c, -(re * s)
                else:
                    a, b = re * c + im * s, im * c - re * s
                spec[k, kind, :, lanes] = a.astype(bf16)
                spec[k, kind, :, lane * 128 + FINE : lane * 128 + FINE + 128] = b.astype(bf16)

    group = 33

    @pl.loop(0, BINS // group)
    def _(step):
        at = pl.ds(step * group, group)
        both = jnp.dot(
            spec[at].reshape(group * 2 * PART, 2 * FINE), forward[...], preferred_element_type=f32
        ).reshape(group, 2, PART, 2 * FINE)
        zr, zi = both[:, 0, :, :FINE], both[:, 0, :, FINE:]
        hr, hi = both[:, 1, :, :FINE], both[:, 1, :, FINE:]
        y = jnp.concatenate([zr * hr - zi * hi, zr * hi + zi * hr], axis=-1).astype(bf16)
        waves[at] = jnp.dot(y.reshape(group * PART, 2 * FINE), back[...], preferred_element_type=f32).reshape(
            group, PART, 2 * FINE
        )

    for lane in range(2):
        lanes = slice(lane * 128, lane * 128 + 128)
        bins = {}
        for k in range(BINS):
            re, im = waves[k, :, lanes], waves[k, :, lane * 128 + FINE : lane * 128 + FINE + 128]
            c, s = twiddle[k, 2:3, lanes], twiddle[k, 3:4, lanes]
            bins[k] = (re * c - im * s, None if k in (0, BINS - 1) else im * c + re * s)
        for p, y in enumerate(half_real_back(bins, 2 * SEQ)):
            conv[lane, part, p] = y.astype(bf16)


def kernel(
    inner_hbm, values_hbm, outer_hbm, filters_hbm, skip_hbm, w_hbm, forward_hbm, back_hbm, twiddle_hbm, out,
    inner, values, outer, filters, skip, w, forward, back, twiddle,
    send, recv, spec, waves, conv, turned, mixed, eye, psend, passed, precv, kept, zsend, zrecv,
    load_sem, send_sem, recv_sem, csend_sem, crecv_sem, rsend_sem, rrecv_sem, psend_sem, precv_sem, zsend_sem, zrecv_sem,
):
    f32 = jnp.float32
    bf16 = jnp.bfloat16
    me, tp = lax.axis_index("seq"), lax.axis_index("tp")
    y, z = tp // 2, lax.rem(tp, 2)
    loads = [
        pltpu.make_async_copy(a, b, load_sem.at[i])
        for i, (a, b) in enumerate((
            (inner_hbm, inner), (values_hbm, values), (filters_hbm, filters), (forward_hbm, forward), (back_hbm, back),
            (twiddle_hbm.at[pl.ds(0, BINS)], twiddle), (outer_hbm, outer), (skip_hbm, skip), (w_hbm, w),
        ))
    ]
    barrier = pltpu.get_barrier_semaphore()

    @pl.loop(1, SEQ)
    def _(i):
        pl.semaphore_signal(barrier, inc=1, device_id={"seq": me ^ i}, device_id_type=MESH)

    for d in (1, 3):
        pl.semaphore_signal(barrier, inc=1, device_id={"tp": lax.rem(y + d, 4) * 2 + z}, device_id_type=MESH)
    pl.semaphore_signal(barrier, inc=1, device_id={"tp": y * 2 + 1 - z}, device_id_type=MESH)
    for load in loads:
        load.start()
    row = lax.broadcasted_iota(jnp.int32, (FINE, FINE), 0)
    col = lax.broadcasted_iota(jnp.int32, (FINE, FINE), 1)
    eye[...] = jnp.where(row == col, 1.0, 0.0).astype(bf16)
    for load in loads[:3]:
        load.wait()

    def spread(part, block):
        @pl.loop(0, 8)
        def _(i):
            peer = block * 8 + (lax.rem(me, 8) ^ (7 - i))

            @pl.when(peer != me)
            def _():
                pltpu.make_async_remote_copy(
                    send.at[part, peer], recv.at[part, me], send_sem.at[part], recv_sem.at[part],
                    device_id={"seq": peer}, device_id_type=MESH,
                ).start()

    def pack(block):
        cols = pl.ds(pl.multiple_of(block * FINE, FINE), FINE)
        product = (inner[:, cols].astype(f32) * values[:, cols].astype(f32)).astype(bf16)
        for kind, piece in enumerate((product, filters[:, cols].astype(bf16))):
            flat = lax.dot_general(eye[...], piece, NT, preferred_element_type=f32).astype(bf16).reshape(8, 2, PART, FINE)
            for part in range(2):
                send[part, pl.ds(block * 8, 8), kind] = flat[:, part]

    first = lax.rem(me // 8 + 1, 4)
    pack(first)
    pl.semaphore_wait(barrier, SEQ + 2)
    spread(0, first)

    @pl.loop(1, 4)
    def _(step):
        block = lax.rem(me // 8 + 1 + step, 4)
        pack(block)
        spread(0, block)

    @pl.loop(0, 4)
    def _(step):
        spread(1, lax.rem(me // 8 + 1 + step, 4))

    for part in range(2):
        recv[part, me] = send[part, me]
    for load in loads[3:6]:
        load.wait()

    def give_back(half, part):
        @pl.loop(1, SEQ)
        def _(i):
            peer = me ^ (SEQ - i)
            pltpu.make_async_remote_copy(
                conv.at[half, part, peer], turned.at[half, part, me], csend_sem.at[half, part], crecv_sem.at[half, part],
                device_id={"seq": peer}, device_id_type=MESH,
            ).start()

        turned[half, part, me] = conv[half, part, me]

    def wait_bytes(ref, sem):
        pltpu.make_async_copy(ref.at[pl.ds(0, SEQ - 1)], ref.at[pl.ds(0, SEQ - 1)], sem).wait()

    @pl.loop(0, 2)
    def _(part):
        wait_bytes(recv.at[part], recv_sem.at[part])

        @pl.when(part == 1)
        def _():
            give_back(0, 0)

        transform(part, recv, forward, back, twiddle, spec, waves, conv)

    give_back(0, 1)
    give_back(1, 0)
    give_back(1, 1)
    for load in loads[6:]:
        load.wait()

    def mix(half):
        for part in range(2):
            wait_bytes(turned.at[half, part], crecv_sem.at[half, part])
        rows = slice(half * 128, half * 128 + 128)

        @pl.loop(0, 4)
        def _(block):
            cols = pl.ds(pl.multiple_of(block * FINE, FINE), FINE)
            both = [turned[half, part, pl.ds(block * 8, 8)].reshape(8, 1, PART, 128) for part in range(2)]
            piece = jnp.concatenate(both, axis=1).reshape(FINE, 128)
            here = lax.dot_general(eye[:128, :128], piece, NT, preferred_element_type=f32)
            product = inner[rows, cols].astype(f32) * values[rows, cols].astype(f32)
            mixed[rows, cols] = (outer[rows, cols].astype(f32) * (here + skip[:, cols] * product)).astype(bf16)

    def beside(step):
        return {"tp": lax.rem(y + 1 + 2 * step, 4) * 2 + z}

    def relay(chunk, step):
        rows = pl.ds(0, CHUNKS[chunk][1])
        return pltpu.make_async_remote_copy(
            psend.at[chunk, 2, step, rows], passed.at[chunk, step, rows], rsend_sem.at[chunk, step], rrecv_sem.at[chunk, step],
            device_id=beside(step), device_id_type=MESH,
        )

    def share(chunk, step, piece):
        rows = pl.ds(0, CHUNKS[chunk][1])
        return pltpu.make_async_remote_copy(
            psend.at[chunk, 1 + 2 * step, piece, rows], precv.at[chunk, step, piece, rows],
            psend_sem.at[chunk, step, piece], precv_sem.at[chunk, step, piece],
            device_id=beside(step), device_id_type=MESH,
        )

    def swap(chunk):
        rows = pl.ds(0, CHUNKS[chunk][1])
        return pltpu.make_async_remote_copy(
            zsend.at[chunk, rows], zrecv.at[chunk, rows], zsend_sem.at[chunk], zrecv_sem.at[chunk],
            device_id={"tp": y * 2 + 1 - z}, device_id_type=MESH,
        )

    def produce(half):
        chunks = [c for c, (start, _) in enumerate(CHUNKS) if start // 128 == half]
        for d in (2, 1, 3, 0):
            target = lax.rem(y + d, 4)

            @pl.loop(0, 2)
            def _(piece):
                cols = pl.ds(pl.multiple_of(target * 1024 + piece * 512, 512), 512)
                part = jnp.dot(
                    mixed[half * 128 : half * 128 + 128, :], w[:, cols], preferred_element_type=f32
                ).astype(bf16)
                for c in chunks:
                    start, count = CHUNKS[c]
                    psend[c, d, piece, 0:count] = part[start - half * 128 : start - half * 128 + count]

            for c in chunks:
                if d == 2:
                    relay(c, 0).start()
                    relay(c, 1).start()
                elif d:
                    share(c, d // 2, 1 - d // 2).start()

    def forward_on(chunk):
        count = CHUNKS[chunk][1]
        for step in range(2):
            relay(chunk, step).wait_recv()
            both = psend[chunk, 1 + 2 * step, step, 0:count].astype(f32) + passed[chunk, step, 0:count].astype(f32)
            psend[chunk, 1 + 2 * step, step, 0:count] = both.astype(bf16)
            share(chunk, step, step).start()

    def add_up(chunk):
        count = CHUNKS[chunk][1]
        for step in range(2):
            for piece in range(2):
                share(chunk, step, piece).wait_recv()

        def total(piece):
            acc = psend[chunk, 0, piece, 0:count].astype(f32)
            for step in range(2):
                acc += precv[chunk, step, piece, 0:count].astype(f32)
            return acc

        zsend[chunk, 0:count] = total(1 - z).astype(bf16)
        swap(chunk).start()
        kept[chunk, 0:count] = total(z)

    def finish(chunk):
        start, count = CHUNKS[chunk]
        swap(chunk).wait()
        out[start : start + count, :] = (kept[chunk, 0:count] + zrecv[chunk, 0:count].astype(f32)).astype(bf16)

    mix(0)
    produce(0)
    forward_on(0)
    forward_on(1)
    mix(1)
    produce(1)
    add_up(0)
    forward_on(2)
    add_up(1)
    forward_on(3)
    add_up(2)
    add_up(3)
    finish(0)
    finish(1)
    finish(2)
    finish(3)
    for chunk in range(len(CHUNKS)):
        for step in range(2):
            relay(chunk, step).wait_send()
            for piece in range(2):
                share(chunk, step, piece).wait_send()
    for part in range(2):
        wait_bytes(send.at[part], send_sem.at[part])
        for half in range(2):
            wait_bytes(conv.at[half, part], csend_sem.at[half, part])


def local(inner_gate, values, outer_gate, filters, skip_gain, w_out):
    f32, bf16 = jnp.float32, jnp.bfloat16
    dma = pltpu.SemaphoreType.DMA
    return pl.pallas_call(
        kernel,
        out_shape=jax.ShapeDtypeStruct((FINE, 512), bf16),
        in_specs=[pl.BlockSpec(memory_space=pl.ANY)] * 9,
        out_specs=pl.BlockSpec(memory_space=pltpu.VMEM),
        scratch_shapes=[
            pltpu.VMEM((FINE, 1024), bf16),
            pltpu.VMEM((FINE, 1024), bf16),
            pltpu.VMEM((FINE, 1024), bf16),
            pltpu.VMEM((FINE, 1024), f32),
            pltpu.VMEM((1, 1024), f32),
            pltpu.VMEM((1024, 4096), bf16),
            pltpu.VMEM((2 * FINE, 2 * FINE), bf16),
            pltpu.VMEM((2 * FINE, 2 * FINE), bf16),
            pltpu.VMEM((BINS, 8, FINE), f32),
            pltpu.VMEM((2, SEQ, 2, PART, FINE), bf16),
            pltpu.VMEM((2, SEQ, 2, PART, FINE), bf16),
            pltpu.VMEM((BINS, 2, PART, 2 * FINE), bf16),
            pltpu.VMEM((BINS, PART, 2 * FINE), f32),
            pltpu.VMEM((2, 2, SEQ, PART, 128), bf16),
            pltpu.VMEM((2, 2, SEQ, PART, 128), bf16),
            pltpu.VMEM((FINE, 1024), bf16),
            pltpu.VMEM((FINE, FINE), bf16),
            pltpu.VMEM((4, 4, 2, 64, 512), bf16),
            pltpu.VMEM((4, 2, 64, 512), bf16),
            pltpu.VMEM((4, 2, 2, 64, 512), bf16),
            pltpu.VMEM((4, 64, 512), f32),
            pltpu.VMEM((4, 64, 512), bf16),
            pltpu.VMEM((4, 64, 512), bf16),
            dma((9,)),
            dma((2,)),
            dma((2,)),
            dma((2, 2)),
            dma((2, 2)),
            dma((4, 2)),
            dma((4, 2)),
            dma((4, 2, 2)),
            dma((4, 2, 2)),
            dma((4,)),
            dma((4,)),
        ],
        compiler_params=pltpu.CompilerParams(collective_id=0, has_side_effects=True, vmem_limit_bytes=56098816),
        name="hyena",
    )(inner_gate, values, outer_gate, filters, skip_gain.reshape(1, -1), w_out, *tables())


def solution(mesh):
    in_specs = (P("seq", "tp"), P("seq", "tp"), P("seq", "tp"), P("seq", "tp"), P("tp"), P("tp", None))
    return jax.shard_map(local, mesh=mesh, in_specs=in_specs, out_specs=P("seq", "tp"), check_vma=False)
```
